512 devices in a mesh: row: 32 (over z, x), col: 16 (over y, core).
Axes of the slice: x: 4, y: 8, z: 8, core: 2. Of those that a mesh axis runs over, the one named last changes fastest.
Arguments:
- activations: bfloat16 [262144, 4096], P(('row', 'col')), may hold values from -110 to 110, as said below
- sketch: bfloat16 [4096, 128], P('col'), may hold values from -0.09375 to 0.09375
Outputs:
- basis: float32 [262144, 128], P(('row', 'col'))
- components: float32 [4096, 128], P('col')
The draws below stay inside these ranges and needn't reach their ends.
Inputs may be any that keep to these rules, and one draw needn't show every extreme that they name: `activations`: rows and features carry different scales.
All inputs are finite; a program needn't handle non-finite values.
Results may differ from the reference program's by a relative error of at most 0.003.
Values may be sent and summed in bfloat16 or wider, within the bound.
A program may use at most 64 MiB of HBM per device.

```python
import jax
import jax.numpy as jnp
from jax import lax

D = 4096
K = 128
ROWS = 262144


def draw_activations(key, part):
    key = jax.random.fold_in(key, 11)
    key_base, key_rows, key_cols = jax.random.split(key, 3)
    base = jnp.clip(jax.random.normal(key_base, (ROWS, D), jnp.float32), -4.0, 4.0)
    col_scale = jnp.exp(jax.random.uniform(key_cols, (1, D), jnp.float32, 0.0, 1.38))
    position = jnp.arange(ROWS, dtype=jnp.float32)[:, None] / jnp.float32(ROWS - 1)
    row_scale = jnp.exp(jax.random.uniform(key_rows, (ROWS, 1), jnp.float32, -0.69, 0.69)) * (1.0 + 2.0 * position)
    return (base * row_scale * col_scale).astype(jnp.bfloat16)


def block_scale(rng, shape, shards, least, top_value):
    level = 1.0
    for dim, blocks in shards:
        heights = jax.random.uniform(jax.random.fold_in(jax.random.fold_in(rng, 6), dim), (blocks,), jnp.float32, least / len(shards), top_value / len(shards))
        level = level * jnp.repeat(jnp.exp(heights), shape[dim] // blocks).reshape((-1,) + (1,) * (len(shape) - 1 - dim))
    return level


def gaussian(stream_key, extent, deviation, reach, cuts=(), held_as=jnp.bfloat16):
    level = block_scale(stream_key, extent, cuts, -0.22, 0.18) if cuts else 1.0
    array = jax.random.normal(stream_key, extent, jnp.float32) * deviation * level
    return jnp.minimum(jnp.maximum(array, -reach), reach).astype(held_as)


def setup_inputs(seed: int = 0) -> dict:
    arg_keys = jax.random.split(jax.random.key(seed), 3)
    return {
        "activations": draw_activations(jax.random.fold_in(arg_keys[2], 71), 0),
        "sketch": gaussian(arg_keys[1], (D, K), D ** -0.5, 0.09375, ((0, 16),)),
    }


def orthonormal(block):
    gram = lax.dot_general(block, block, (((0,), (0,)), ((), ())), precision=lax.Precision.HIGHEST)
    lower = jnp.linalg.cholesky(gram)
    return lax.linalg.triangular_solve(lower, block, left_side=False, lower=True, transpose_a=True)

def reference(activations, sketch):
    first = jnp.dot(activations.astype(jnp.float32), sketch.astype(jnp.float32), preferred_element_type=jnp.float32)
    ortho_one = orthonormal(first)
    data_wide = activations.astype(jnp.float32)
    coeffs = lax.dot_general(data_wide, ortho_one, (((0,), (0,)), ((), ())), precision=lax.Precision.HIGHEST)
    second = jnp.dot(data_wide, coeffs, precision=lax.Precision.HIGHEST)
    ortho_two = orthonormal(second)
    scale_root = jnp.sqrt(jnp.float32(ROWS))
    basis = ortho_two * scale_root
    projected = lax.dot_general(data_wide, ortho_two, (((0,), (0,)), ((), ())), precision=lax.Precision.HIGHEST)
    return (basis, projected / scale_root)
```

```python
import math

import jax
import jax.numpy as jnp
from jax import lax
from jax.experimental import pallas as pl
from jax.experimental.pallas import tpu as pltpu
from jax.sharding import PartitionSpec as P

f32, bf16 = jnp.float32, jnp.bfloat16
NX, NY, NZ = 4, 8, 8
K, BLOCK, ROWS = 128, 256, 512
NT = (((1,), (1,)), ((), ()))
RING8 = (4, 3, 5, 2, 6, 1, 7)
RING4 = (2, 1, 3)


def split2(value):
    high = value.astype(bf16)
    return high, (value - high.astype(f32)).astype(bf16)


def split3(value):
    high = value.astype(bf16)
    rest = value - high.astype(f32)
    middle = rest.astype(bf16)
    return high, middle, (rest - middle.astype(f32)).astype(bf16)


def times_transposed(left, right):
    lh, ll = split2(left)
    rh, rl = split2(right)
    return lax.dot_general(
        jnp.concatenate([lh, ll, lh], axis=1),
        jnp.concatenate([rh, rh, rl], axis=1),
        NT,
        preferred_element_type=f32,
    )


def cholesky_stage(b, work):
    base = pl.multiple_of(b * 8, 8)
    panel = work[pl.ds(base, 8), :]
    g, w = panel[:, :K], panel[:, K:]
    lane = lax.broadcasted_iota(jnp.int32, (8, K), 1)
    sub = lax.broadcasted_iota(jnp.int32, (8, K), 0)
    pivots = [
        jnp.broadcast_to(jnp.sum(jnp.where(lane == base + k, g, 0.0), axis=1, keepdims=True), (8, K)) for k in range(8)
    ]
    for i in range(8):
        d = jnp.broadcast_to(pivots[i][i : i + 1], (8, K))
        r = lax.rsqrt(d)
        r = r * (1.5 - 0.5 * d * r * r)
        low = jnp.where(sub > i, pivots[i] * r, 0.0)
        keep = sub == i
        gi = jnp.broadcast_to(g[i : i + 1], (8, K)) * r
        wi = jnp.broadcast_to(w[i : i + 1], (8, K)) * r
        g = jnp.where(keep, gi, g - low * gi)
        w = jnp.where(keep, wi, w - low * wi)
        for k in range(i + 1, 8):
            pivots[k] = pivots[k] - low * (jnp.broadcast_to(pivots[k][i : i + 1], (8, K)) * r)
    rows = jnp.concatenate([g, w], axis=1)
    work[pl.ds(base, 8), :] = rows
    left = split3(jnp.where(lane >= base + 8, g, 0.0))
    right = split3(rows)
    pairs = ((0, 0), (0, 1), (1, 0), (1, 1), (0, 2), (2, 0))
    work[...] -= lax.dot_general(
        jnp.concatenate([left[i] for i, _ in pairs], axis=0),
        jnp.concatenate([right[j] for _, j in pairs], axis=0),
        (((0,), (0,)), ((), ())),
        preferred_element_type=f32,
    )


def kernel(
    a_hbm, s_in, sec, w_out, ct_out,
    a_v, s_v, f_acc, ft, work, acc,
    g_local, g_core, g_sum, g_y, g_z, g_x, g_all,
    c_send, c_recv, c_own,
    y1s, z1s, x1s, y1r, z1r, x1r,
    y2s, z2s, x2s, y2r, z2r, x2r,
    y3, z3, x3, f_y, f_z, f_x, e_y, e_z, e_x,
    load_sem, s_send, s_recv, p_recv, send_sems, recv_sems,
):
    row, col = lax.axis_index("row"), lax.axis_index("col")
    z, x, y, h = row // NX, lax.rem(row, NX), col // 2, lax.rem(col, 2)
    other = 1 - h

    def at(zz, xx, yy, hh):
        return (zz * NX + xx, yy * 2 + hh)

    def ring(axis):
        if axis == "y":
            return [(d, lax.rem(y + d, NY), at(z, x, lax.rem(y + d, NY), h)) for d in RING8]
        if axis == "z":
            return [(d, lax.rem(z + d, NZ), at(lax.rem(z + d, NZ), x, y, h)) for d in RING8]
        return [(d, lax.rem(x + d, NX), at(z, lax.rem(x + d, NX), y, h)) for d in RING4]

    partner = at(z, x, y, other)
    pending = []
    slots = {}

    def slot(name):
        return slots.setdefault(name, len(slots))

    def copy_to(name, device, src, dst):
        i = slot(name)
        pltpu.make_async_remote_copy(
            src_ref=src, dst_ref=dst, send_sem=send_sems.at[i], recv_sem=recv_sems.at[i],
            device_id=device, device_id_type=pl.DeviceIdType.MESH,
        ).start()

    def arrived(name, ref):
        pltpu.make_async_copy(ref, ref, recv_sems.at[slot(name)]).wait()
        pending.append((slot(name), ref))

    def scatter(name, axis, src, dst):
        for d, place, device in ring(axis):
            copy_to(name, device, src.at[place], dst.at[d - 1])

    def spread(name, axis, ref):
        for _, _, device in ring(axis):
            copy_to(name, device, ref, ref)

    loads = [
        pltpu.make_async_copy(
            a_hbm.at[:, pl.ds((yy * 2 + hh) * BLOCK, BLOCK)], a_v.at[hh, yy], load_sem.at[0]
        )
        for hh in range(2)
        for yy in range(NY)
    ]
    for load in loads:
        load.start()
    barrier = pltpu.get_barrier_semaphore()
    peers = [partner] + [device for axis in "yzx" for _, _, device in ring(axis)]
    for device in peers:
        pl.semaphore_signal(barrier, inc=1, device_id=device, device_id_type=pl.DeviceIdType.MESH)
    s_v[h, y] = s_in[...]
    pl.semaphore_wait(barrier, len(peers))

    def sketch_copy(src, dst, device, i, recv):
        return pltpu.make_async_remote_copy(
            src_ref=src, dst_ref=dst, send_sem=s_send.at[i], recv_sem=recv.at[i],
            device_id=device, device_id_type=pl.DeviceIdType.MESH,
        )

    mine = s_v.at[h, y]
    for d in (1, 7, 2, 6, 3, 5, 4):
        sketch_copy(mine, mine, at(z, x, lax.rem(y + d, NY), h), d, s_recv).start()

    def hand_on(d, place):
        block = s_v.at[h, place]
        pltpu.make_async_remote_copy(
            src_ref=block, dst_ref=block, send_sem=s_send.at[8 + d], recv_sem=p_recv.at[d],
            device_id=partner, device_id_type=pl.DeviceIdType.MESH,
        ).start()

    def distance(i):
        half = (i + 1) // 2
        return jnp.where(lax.rem(i, 2) == 1, half, lax.rem(NY - half, NY))

    hand_on(0, y)
    pltpu.make_async_copy(a_v, a_v, load_sem.at[0]).wait()
    f_acc[...] = jnp.dot(a_v[h, y], s_v[h, y], preferred_element_type=f32)

    @pl.loop(1, NY)
    def _(i):
        d = distance(i)
        place = lax.rem(y + NY - d, NY)
        block = s_v.at[h, place]
        pltpu.make_async_copy(block, block, s_recv.at[d]).wait()
        hand_on(d, place)
        f_acc[...] += jnp.dot(a_v[h, place], block[...], preferred_element_type=f32)

    @pl.loop(0, NY)
    def _(i):
        d = distance(i)
        place = lax.rem(y + NY - d, NY)
        block = s_v.at[other, place]
        pltpu.make_async_copy(block, block, p_recv.at[d]).wait()
        f_acc[...] += jnp.dot(a_v[other, place], block[...], preferred_element_type=f32)

    def project(p, tall):
        high, low = split2(tall.T)
        ft[:K, :] = high
        ft[K:, :] = low
        both = ft[...]
        square = lax.dot_general(both, both, NT, preferred_element_type=f32)
        gram = (square[:K, :K] + square[K:, K:]) + (square[:K, K:] + square[K:, :K])
        g_local[p] = gram.reshape(2, 8, 8, K)
        copy_to(f"gc{p}", partner, g_local.at[p, other], g_core.at[p])

        @pl.loop(0, NY)
        def _(i):
            both = jnp.dot(ft[...], a_v[other, i], preferred_element_type=f32)
            c_send[p, i] = (both[:K] + both[K:]).astype(bf16)
            copy_to(f"c{p}", partner, c_send.at[p, i], c_recv.at[p, i])

        @pl.loop(0, NY)
        def _(i):
            both = jnp.dot(ft[...], a_v[h, i], preferred_element_type=f32)
            c_own[i] = both[:K] + both[K:]

    def gram_y(p):
        arrived(f"gc{p}", g_core.at[p])
        g_sum[p] = g_local[p, h] + g_core[p]
        scatter(f"gy{p}", "y", g_sum.at[p], g_y.at[p])

    def gram_z(p):
        arrived(f"gy{p}", g_y.at[p])
        g_z[p, z] = g_sum[p, y] + jnp.sum(g_y[p], axis=0)
        spread(f"gz{p}", "z", g_z.at[p, z])

    def gram_x(p):
        arrived(f"gz{p}", g_z.at[p, pl.ds(0, NZ - 1)])
        g_x[p, x] = jnp.sum(g_z[p], axis=0)
        spread(f"gx{p}", "x", g_x.at[p, x])

    def gram_back_y(p):
        arrived(f"gx{p}", g_x.at[p, pl.ds(0, NX - 1)])
        g_all[p, h, y] = jnp.sum(g_x[p], axis=0)
        spread(f"ga{p}", "y", g_all.at[p, h, y])

    def gram_back_core(p):
        arrived(f"ga{p}", g_all.at[p, h, pl.ds(0, NY - 1)])
        copy_to(f"gb{p}", partner, g_all.at[p, h], g_all.at[p, h])

    def gram_done(p):
        arrived(f"gb{p}", g_all.at[p, other])
        ri = lax.broadcasted_iota(jnp.int32, (K, K), 0)
        ci = lax.broadcasted_iota(jnp.int32, (K, K), 1)
        work[:, :K] = g_all[p].reshape(K, K)
        work[:, K:] = jnp.where(ri == ci, 1.0, 0.0)

    def stages(lo, hi):
        @pl.loop(lo, hi)
        def _(b):
            cholesky_stage(b, work)

    def one(p):
        arrived(f"c{p}", c_recv.at[p])

        @pl.loop(0, NY // 2)
        def _(j):
            even = c_own[2 * j] + c_recv[p, 2 * j].astype(f32)
            odd = c_own[2 * j + 1] + c_recv[p, 2 * j + 1].astype(f32)
            for place, value in ((2 * j, even), (2 * j + 1, odd)):
                y1s[p, place] = value[:32].astype(bf16)
                for q in range(NX):
                    x1s[p, q, place] = value[64 + 16 * q : 80 + 16 * q].astype(bf16)
            for q in range(NZ):
                r, c = 32 + 8 * (q // 2), K * (q % 2)
                tiles = [value[r : r + 8, c : c + K] for value in (even, odd)]
                z1s[p, q, pl.ds(pl.multiple_of(j * 16, 16), 16)] = jnp.concatenate(tiles, axis=0).astype(bf16)

        scatter(f"y1{p}", "y", y1s.at[p], y1r.at[p])
        scatter(f"z1{p}", "z", z1s.at[p], z1r.at[p])
        scatter(f"x1{p}", "x", x1s.at[p], x1r.at[p])

    def total(own, parts):
        return own.astype(f32) + jnp.sum(parts.astype(f32), axis=0)

    def two(p):
        arrived(f"y1{p}", y1r.at[p])
        value = total(y1s[p, y], y1r[p])
        for q in range(NZ):
            y2s[p, q] = value[8 * (q // 2) : 8 * (q // 2) + 8, K * (q % 2) : K * (q % 2) + K]
        scatter(f"y2{p}", "z", y2s.at[p], y2r.at[p])
        arrived(f"z1{p}", z1r.at[p])
        z2s[p] = total(z1s[p, z], z1r[p]).reshape(NY, 8, K)
        scatter(f"z2{p}", "y", z2s.at[p], z2r.at[p])
        arrived(f"x1{p}", x1r.at[p])
        x2s[p] = total(x1s[p, x], x1r[p])
        scatter(f"x2{p}", "y", x2s.at[p], x2r.at[p])

    def three(p):
        arrived(f"y2{p}", y2r.at[p])
        y3[p, x] = total(y2s[p, z], y2r[p])
        spread(f"y3{p}", "x", y3.at[p, x])
        arrived(f"z2{p}", z2r.at[p])
        z3[p, x] = total(z2s[p, y], z2r[p])
        spread(f"z3{p}", "x", z3.at[p, x])
        arrived(f"x2{p}", x2r.at[p])
        x3[p, z] = total(x2s[p, y], x2r[p])
        spread(f"x3{p}", "z", x3.at[p, z])

    def sums(p):
        arrived(f"y3{p}", y3.at[p, pl.ds(0, NX - 1)])
        yield jnp.sum(y3[p], axis=0)
        arrived(f"z3{p}", z3.at[p, pl.ds(0, NX - 1)])
        yield jnp.sum(z3[p], axis=0)
        arrived(f"x3{p}", x3.at[p, pl.ds(0, NZ - 1)])
        yield jnp.sum(x3[p], axis=0)

    project(0, f_acc[...])
    gram_y(0)
    one(0)
    gram_z(0)
    two(0)
    gram_x(0)
    three(0)
    gram_back_y(0)
    gather = sums(0)
    f_y[h, y, z] = next(gather)
    spread("y4", "z", f_y.at[h, y, z])
    f_z[h, z, y] = next(gather)
    spread("z4", "y", f_z.at[h, z, y])
    f_x[h, x, y] = next(gather)
    spread("x4", "y", f_x.at[h, x, y])
    next(gather, None)
    gram_back_core(0)
    arrived("y4", f_y.at[h, y, pl.ds(0, NZ - 1)])
    spread("y5", "y", f_y.at[h, y])
    arrived("z4", f_z.at[h, z, pl.ds(0, NY - 1)])
    spread("z5", "z", f_z.at[h, z])
    arrived("x4", f_x.at[h, x, pl.ds(0, NY - 1)])
    spread("x5", "x", f_x.at[h, x])
    gram_done(0)
    stages(0, 16)
    arrived("y5", f_y.at[h, pl.ds(0, NY - 1)])
    copy_to("y6", partner, f_y.at[h], f_y.at[h])
    arrived("z5", f_z.at[h, pl.ds(0, NZ - 1)])
    copy_to("z6", partner, f_z.at[h], f_z.at[h])
    arrived("x5", f_x.at[h, pl.ds(0, NX - 1)])
    copy_to("x6", partner, f_x.at[h], f_x.at[h])

    def tiles(ref):
        rows = [jnp.concatenate([ref[2 * k], ref[2 * k + 1]], axis=1) for k in range(4)]
        return jnp.concatenate(rows, axis=0)

    def second_part(half):
        @pl.loop(0, NY)
        def _(i):
            parts = [tiles(f_y.at[half, i])]
            parts += [tiles(f_z.at[half, :, i])]
            parts += [f_x[half, q, i] for q in range(NX)]
            high, low = split2(jnp.concatenate(parts, axis=0))
            acc[...] += lax.dot_general(
                a_v[half, i], jnp.concatenate([high, low], axis=0), NT, preferred_element_type=f32
            )

    acc[...] = jnp.zeros_like(acc)
    second_part(h)
    arrived("y6", f_y.at[other])
    arrived("z6", f_z.at[other])
    arrived("x6", f_x.at[other])
    second_part(other)
    sec[...] = times_transposed(acc[:, :K] + acc[:, K:], work[:, K:])

    project(1, sec[...])
    gram_y(1)
    one(1)
    gram_z(1)
    two(1)
    gram_x(1)
    three(1)
    gram_back_y(1)
    gather = sums(1)
    e_y[z] = next(gather)
    spread("y7", "z", e_y.at[z])
    e_z[z] = next(gather)
    spread("z7", "z", e_z.at[z])
    e_x[x] = next(gather)
    spread("x7", "x", e_x.at[x])
    next(gather, None)
    gram_back_core(1)
    gram_done(1)
    stages(0, 16)
    w_out[...] = work[:, K:]
    arrived("y7", e_y.at[pl.ds(0, NZ - 1)])
    arrived("z7", e_z.at[pl.ds(0, NZ - 1)])
    arrived("x7", e_x.at[pl.ds(0, NX - 1)])
    ct_out[...] = jnp.concatenate([tiles(e_y), tiles(e_z)] + [e_x[q] for q in range(NX)], axis=0)

    for i, ref in pending:
        pltpu.make_async_copy(ref, ref, send_sems.at[i]).wait()
    for i in range(1, NY):
        pltpu.make_async_copy(mine, mine, s_send.at[i]).wait()
    for i in range(NY):
        pltpu.make_async_copy(mine, mine, s_send.at[8 + i]).wait()


def finish(scale_root, sec, w, ct, basis, components):
    basis[...] = times_transposed(sec[...], w[...]) * scale_root
    components[...] = times_transposed(ct[...].T, w[...]) / scale_root


def on_device(activations, sketch):
    rows_total = activations.shape[0] * lax.axis_size("row") * lax.axis_size("col")
    vmem = pltpu.VMEM
    shapes = [
        vmem((2, NY, ROWS, BLOCK), bf16), vmem((2, NY, BLOCK, K), bf16), vmem((ROWS, K), f32),
        vmem((2 * K, ROWS), bf16), vmem((K, 2 * K), f32), vmem((ROWS, 2 * K), f32),
        vmem((2, 2, 8, 8, K), f32), vmem((2, 8, 8, K), f32), vmem((2, 8, 8, K), f32), vmem((2, NY - 1, 8, K), f32),
        vmem((2, NZ, 8, K), f32), vmem((2, NX, 8, K), f32), vmem((2, 2, 8, 8, K), f32),
        vmem((2, NY, K, BLOCK), bf16), vmem((2, NY, K, BLOCK), bf16), vmem((NY, K, BLOCK), f32),
        vmem((2, NY, 32, BLOCK), bf16), vmem((2, NZ, 64, K), bf16), vmem((2, NX, NY, 16, BLOCK), bf16),
        vmem((2, NY - 1, 32, BLOCK), bf16), vmem((2, NZ - 1, 64, K), bf16), vmem((2, NX - 1, NY, 16, BLOCK), bf16),
        vmem((2, NZ, 8, K), f32), vmem((2, NY, 8, K), f32), vmem((2, NY, 16, BLOCK), f32),
        vmem((2, NZ - 1, 8, K), f32), vmem((2, NY - 1, 8, K), f32), vmem((2, NY - 1, 16, BLOCK), f32),
        vmem((2, NX, 8, K), f32), vmem((2, NX, 8, K), f32), vmem((2, NZ, 16, BLOCK), f32),
        vmem((2, NY, NZ, 8, K), f32), vmem((2, NZ, NY, 8, K), f32), vmem((2, NX, NY, 16, BLOCK), f32),
        vmem((NZ, 8, K), f32), vmem((NZ, 8, K), f32), vmem((NX, 16, BLOCK), f32),
        pltpu.SemaphoreType.DMA((1,)), pltpu.SemaphoreType.DMA((16,)), pltpu.SemaphoreType.DMA((8,)),
        pltpu.SemaphoreType.DMA((8,)), pltpu.SemaphoreType.DMA((48,)), pltpu.SemaphoreType.DMA((48,)),
    ]
    here = pl.BlockSpec(memory_space=pltpu.VMEM)
    sec, w, ct = pl.pallas_call(
        kernel,
        out_shape=(
            jax.ShapeDtypeStruct((ROWS, K), f32),
            jax.ShapeDtypeStruct((K, K), f32),
            jax.ShapeDtypeStruct((K, BLOCK), f32),
        ),
        in_specs=[pl.BlockSpec(memory_space=pl.ANY), here],
        out_specs=(here, here, here),
        scratch_shapes=shapes,
        compiler_params=pltpu.CompilerParams(
            collective_id=0, has_side_effects=True, vmem_limit_bytes=48 << 20
        ),
        name="subspace",
    )(activations, sketch)

    def last(*refs):
        finish(math.sqrt(rows_total), *refs)

    return pl.pallas_call(
        last,
        out_shape=(jax.ShapeDtypeStruct((ROWS, K), f32), jax.ShapeDtypeStruct((BLOCK, K), f32)),
        in_specs=[here, here, here],
        out_specs=(here, here),
        name="outputs",
    )(sec, w, ct)


def solution(mesh):
    placed = (P(("row", "col"), None), P("col", None))
    return jax.shard_map(
        on_device,
        mesh=mesh,
        in_specs=placed,
        out_specs=(P(("row", "col"), None), P("col", None)),
        check_vma=False,
    )
```

```python
import functools
import math

import jax
import jax.numpy as jnp
from jax import lax
from jax.experimental import pallas as pl
from jax.experimental.pallas import tpu as pltpu
from jax.sharding import PartitionSpec as P

f32, bf16 = jnp.float32, jnp.bfloat16
NX, NY, NZ = 4, 8, 8
K, BLOCK, ROWS = 128, 256, 512
PIVOTS = 16
QUARTER = BLOCK // NX
NT = (((1,), (1,)), ((), ()))
RING8 = (4, 3, 5, 2, 6, 1, 7)
RING4 = (2, 1, 3)
NEAR, FAR = (1, 7, 2, 6), (4, 3, 5)
COL16 = (8, 7, 9, 6, 10, 5, 11, 4, 12, 3, 13, 2, 14, 1, 15)


def split2(value):
    high = value.astype(bf16)
    return high, (value - high.astype(f32)).astype(bf16)


def split3(value):
    high = value.astype(bf16)
    rest = value - high.astype(f32)
    middle = rest.astype(bf16)
    return high, middle, (rest - middle.astype(f32)).astype(bf16)


def times_transposed(left, right):
    lh, ll = split2(left)
    rh, rl = split2(right)
    return lax.dot_general(
        jnp.concatenate([lh, ll, lh], axis=1),
        jnp.concatenate([rh, rh, rl], axis=1),
        NT,
        preferred_element_type=f32,
    )


def cholesky_stage(b, work):
    base = pl.multiple_of(b * PIVOTS, PIVOTS)
    panel = work[pl.ds(base, PIVOTS), :]
    g, w = panel[:, :K], panel[:, K:]
    shape = (PIVOTS, K)
    lane = lax.broadcasted_iota(jnp.int32, shape, 1)
    sub = lax.broadcasted_iota(jnp.int32, shape, 0)

    def column(k):
        return jnp.broadcast_to(jnp.sum(jnp.where(lane == base + k, g, 0.0), axis=1, keepdims=True), shape)

    def row(value, i):
        return jnp.broadcast_to(value[i : i + 1], shape)

    pivots = [column(k) for k in range(PIVOTS)]
    for i in range(PIVOTS):
        r = lax.rsqrt(row(pivots[i], i))
        low = jnp.where(sub > i, pivots[i] * r, 0.0)
        gi, wi = row(g, i) * r, row(w, i) * r
        g = jnp.where(sub == i, gi, g - low * gi)
        w = jnp.where(sub == i, wi, w - low * wi)
        for k in range(i + 1, PIVOTS):
            pivots[k] = pivots[k] - low * (row(pivots[k], i) * r)
    rows = jnp.concatenate([g, w], axis=1)
    work[pl.ds(base, PIVOTS), :] = rows
    left = split3(jnp.where(lane >= base + PIVOTS, g, 0.0))
    right = split3(rows)
    pairs = ((0, 0), (0, 1), (1, 0), (1, 1), (0, 2), (2, 0))
    work[...] -= lax.dot_general(
        jnp.concatenate([left[i] for i, _ in pairs], axis=0),
        jnp.concatenate([right[j] for _, j in pairs], axis=0),
        (((0,), (0,)), ((), ())),
        preferred_element_type=f32,
    )


def kernel(
    scale_root, a_hbm, s_hbm, basis, components,
    sec, a_v, s_v, f_acc, ft, work, acc,
    g_local, g_col, g_z, g_x, g_all,
    c_send, c_recv,
    y1s, z1s, x1s, y1r, z1r, x1r,
    y2s, z2s, x2s, y2r, z2r, x2r,
    y3, z3, x3, f_y, f_z, f_x, e_y, e_z, e_x,
    load_sem, s_send, s_recv, p_recv, q_send, q_recv, c_sems, f_sems, send_sems, recv_sems,
):
    row, col = lax.axis_index("row"), lax.axis_index("col")
    z, x, y, h = row // NX, lax.rem(row, NX), col // 2, lax.rem(col, 2)
    other = 1 - h

    def at(zz, xx, yy, hh):
        return (zz * NX + xx, yy * 2 + hh)

    def ring(axis):
        if axis == "y":
            return [(d, lax.rem(y + d, NY), at(z, x, lax.rem(y + d, NY), h)) for d in RING8]
        if axis == "col":
            spots = [lax.rem(col + d, 2 * NY) for d in COL16]
            return [(d, c, (row, c)) for d, c in zip(COL16, spots)]
        if axis == "z":
            return [(d, lax.rem(z + d, NZ), at(lax.rem(z + d, NZ), x, y, h)) for d in RING8]
        return [(d, lax.rem(x + d, NX), at(z, lax.rem(x + d, NX), y, h)) for d in RING4]

    partner = at(z, x, y, other)
    pending = []
    slots = {}

    def slot(name):
        return slots.setdefault(name, len(slots))

    def copy_to(name, device, src, dst):
        i = slot(name)
        pltpu.make_async_remote_copy(
            src_ref=src, dst_ref=dst, send_sem=send_sems.at[i], recv_sem=recv_sems.at[i],
            device_id=device, device_id_type=pl.DeviceIdType.MESH,
        ).start()

    def arrived(name, ref):
        pltpu.make_async_copy(ref, ref, recv_sems.at[slot(name)]).wait()
        pending.append((slot(name), ref))

    def scatter(name, axis, src, dst):
        for d, place, device in ring(axis):
            copy_to(name, device, src.at[place], dst.at[d - 1])

    def spread(name, axis, ref):
        for _, _, device in ring(axis):
            copy_to(name, device, ref, ref)

    loads = [
        pltpu.make_async_copy(
            a_hbm.at[:, pl.ds((yy * 2 + hh) * BLOCK, BLOCK)], a_v.at[hh, yy], load_sem.at[0]
        )
        for hh in range(2)
        for yy in range(NY)
    ]
    own_sketch = pltpu.make_async_copy(s_hbm, s_v.at[h, y], load_sem.at[1])
    own_sketch.start()
    for load in loads:
        load.start()
    barrier = pltpu.get_barrier_semaphore()
    peers = [device for axis in ("col", "z", "x") for _, _, device in ring(axis)]
    for device in peers:
        pl.semaphore_signal(barrier, inc=1, device_id=device, device_id_type=pl.DeviceIdType.MESH)
    own_sketch.wait()
    pl.semaphore_wait(barrier, len(peers))

    def sketch_copy(block, device, sends, recvs, d):
        return pltpu.make_async_remote_copy(
            src_ref=block, dst_ref=block, send_sem=sends, recv_sem=recvs.at[d],
            device_id=device, device_id_type=pl.DeviceIdType.MESH,
        )

    mine = s_v.at[h, y]
    span = pl.ds(pl.multiple_of(x * QUARTER, QUARTER), QUARTER)
    for d in FAR:
        sketch_copy(s_v.at[h, y, span], at(z, x, lax.rem(y + d, NY), h), s_send.at[d], q_recv, d).start()
    for d in NEAR:
        sketch_copy(mine, at(z, x, lax.rem(y + d, NY), h), s_send.at[d], s_recv, d).start()

    def hand_on(d, place):
        sketch_copy(s_v.at[h, place], partner, s_send.at[8 + d], p_recv, d).start()

    def distance(i):
        half = (i + 1) // 2
        return jnp.where(lax.rem(i, 2) == 1, half, lax.rem(NY - half, NY))

    def come(lo, hi, size):
        @pl.loop(lo, hi)
        def _(i):
            d = distance(i)
            place = lax.rem(y + NY - d, NY)
            block = s_v.at[h, place]
            part = s_v.at[h, place, pl.ds(0, size)]
            pltpu.make_async_copy(part, part, s_recv.at[d]).wait()
            hand_on(d, place)
            f_acc[...] += jnp.dot(a_v[h, place], block[...], preferred_element_type=f32)

    hand_on(0, y)
    pltpu.make_async_copy(a_v, a_v, load_sem.at[0]).wait()
    f_acc[...] = jnp.dot(a_v[h, y], s_v[h, y], preferred_element_type=f32)
    come(1, 3, BLOCK)
    for d in FAR:
        quarter = s_v.at[h, lax.rem(y + NY - d, NY), span]
        pltpu.make_async_copy(quarter, quarter, q_recv.at[d]).wait()
        for _, _, device in ring("x"):
            sketch_copy(quarter, device, q_send.at[d], s_recv, d).start()
    come(3, 5, BLOCK)
    come(5, 8, BLOCK - QUARTER)

    @pl.loop(0, NY)
    def _(i):
        d = distance(i)
        place = lax.rem(y + NY - d, NY)
        block = s_v.at[other, place]
        pltpu.make_async_copy(block, block, p_recv.at[d]).wait()
        f_acc[...] += jnp.dot(a_v[other, place], block[...], preferred_element_type=f32)

    def project(p, tall):
        high, low = split2(tall.T)
        ft[:K, :] = high
        ft[K:, :] = low
        both = ft[...]
        square = lax.dot_general(both, both, NT, preferred_element_type=f32)
        gram = (square[:K, :K] + square[K:, K:]) + (square[:K, K:] + square[K:, :K])
        g_local[p] = gram.reshape(2 * NY, 8, K)
        scatter(f"gc{p}", "col", g_local.at[p], g_col.at[p])

        @pl.loop(0, NY // 2)
        def _(j):
            for i in (2 * j, 2 * j + 1):
                both = jnp.dot(ft[...], a_v[other, i], preferred_element_type=f32)
                c_send[p, i] = (both[:K] + both[K:]).astype(bf16)
            pair = pl.ds(2 * j, 2)
            pltpu.make_async_remote_copy(
                src_ref=c_send.at[p, pair], dst_ref=c_recv.at[p, pair],
                send_sem=c_sems.at[p, 0, j], recv_sem=c_sems.at[p, 1, j],
                device_id=partner, device_id_type=pl.DeviceIdType.MESH,
            ).start()

        @pl.loop(0, NY // 2)
        def _(j):
            values = []
            for i in (2 * j, 2 * j + 1):
                both = jnp.dot(ft[...], a_v[h, i], preferred_element_type=f32)
                values.append(both[:K] + both[K:])
            pair = c_recv.at[p, pl.ds(2 * j, 2)]
            pltpu.make_async_copy(pair, pair, c_sems.at[p, 1, j]).wait()
            values = [value + pair[i].astype(f32) for i, value in enumerate(values)]
            for place, value in zip((2 * j, 2 * j + 1), values):
                y1s[p, place] = value[:32].astype(bf16)
                for q in range(NX):
                    x1s[p, q, place] = value[64 + 16 * q : 80 + 16 * q].astype(bf16)
            for q in range(NZ):
                r, c = 32 + 8 * (q // 2), K * (q % 2)
                both = jnp.concatenate([value[r : r + 8, c : c + K] for value in values], axis=0)
                z1s[p, q, pl.ds(pl.multiple_of(j * 16, 16), 16)] = both.astype(bf16)

        scatter(f"x1{p}", "x", x1s.at[p], x1r.at[p])
        scatter(f"y1{p}", "y", y1s.at[p], y1r.at[p])
        scatter(f"z1{p}", "z", z1s.at[p], z1r.at[p])

    def gram_z(p):
        arrived(f"gc{p}", g_col.at[p])
        g_z[p, z] = g_local[p, col] + jnp.sum(g_col[p], axis=0)
        spread(f"gz{p}", "z", g_z.at[p, z])

    def gram_x(p):
        arrived(f"gz{p}", g_z.at[p, pl.ds(0, NZ - 1)])
        g_x[p, x] = jnp.sum(g_z[p], axis=0)
        spread(f"gx{p}", "x", g_x.at[p, x])

    def gram_back(p):
        arrived(f"gx{p}", g_x.at[p, pl.ds(0, NX - 1)])
        g_all[p, col] = jnp.sum(g_x[p], axis=0)
        spread(f"ga{p}", "col", g_all.at[p, col])

    def gram_done(p):
        arrived(f"ga{p}", g_all.at[p, pl.ds(0, 2 * NY - 1)])
        ri = lax.broadcasted_iota(jnp.int32, (K, K), 0)
        ci = lax.broadcasted_iota(jnp.int32, (K, K), 1)
        work[:, :K] = g_all[p].reshape(K, K)
        work[:, K:] = jnp.where(ri == ci, 1.0, 0.0)

    def stages(lo, hi):
        @pl.loop(lo, hi)
        def _(b):
            cholesky_stage(b, work)

    def total(own, parts):
        return own.astype(f32) + jnp.sum(parts.astype(f32), axis=0)

    def two(p):
        arrived(f"x1{p}", x1r.at[p])
        x2s[p] = total(x1s[p, x], x1r[p]).astype(bf16)
        scatter(f"x2{p}", "y", x2s.at[p], x2r.at[p])
        arrived(f"y1{p}", y1r.at[p])
        value = total(y1s[p, y], y1r[p])
        for q in range(NZ):
            y2s[p, q] = value[8 * (q // 2) : 8 * (q // 2) + 8, K * (q % 2) : K * (q % 2) + K]
        scatter(f"y2{p}", "z", y2s.at[p], y2r.at[p])
        arrived(f"z1{p}", z1r.at[p])
        z2s[p] = total(z1s[p, z], z1r[p]).reshape(NY, 8, K)
        scatter(f"z2{p}", "y", z2s.at[p], z2r.at[p])

    def three(p):
        arrived(f"y2{p}", y2r.at[p])
        y3[p, x] = total(y2s[p, z], y2r[p])
        spread(f"y3{p}", "x", y3.at[p, x])
        arrived(f"z2{p}", z2r.at[p])
        z3[p, x] = total(z2s[p, y], z2r[p])
        spread(f"z3{p}", "x", z3.at[p, x])
        arrived(f"x2{p}", x2r.at[p])
        x3[p, z] = total(x2s[p, y], x2r[p])
        spread(f"x3{p}", "z", x3.at[p, z])

    def sums(p):
        arrived(f"y3{p}", y3.at[p, pl.ds(0, NX - 1)])
        yield jnp.sum(y3[p], axis=0)
        arrived(f"z3{p}", z3.at[p, pl.ds(0, NX - 1)])
        yield jnp.sum(z3[p], axis=0)
        arrived(f"x3{p}", x3.at[p, pl.ds(0, NZ - 1)])
        yield jnp.sum(x3[p], axis=0)

    project(0, f_acc[...])
    gram_z(0)
    gram_x(0)
    two(0)
    gram_back(0)
    three(0)
    gather = sums(0)
    f_y[h, y, z] = next(gather)
    spread("y4", "z", f_y.at[h, y, z])
    f_z[h, z, y] = next(gather)
    spread("z4", "y", f_z.at[h, z, y])
    f_x[h, x, y] = next(gather)
    spread("x4", "y", f_x.at[h, x, y])
    gram_done(0)
    arrived("y4", f_y.at[h, y, pl.ds(0, NZ - 1)])
    arrived("z4", f_z.at[h, z, pl.ds(0, NY - 1)])
    arrived("x4", f_x.at[h, x, pl.ds(0, NY - 1)])

    def fanned(i, block, device):
        pltpu.make_async_remote_copy(
            src_ref=block, dst_ref=block, send_sem=f_sems.at[0, i], recv_sem=f_sems.at[1, i],
            device_id=device, device_id_type=pl.DeviceIdType.MESH,
        ).start()

    for k, (d, _, device) in enumerate(ring("y")):
        fanned(d, f_y.at[h, y], device)
        fanned(8 + d, f_z.at[h, z], ring("z")[k][2])
        if k < NX - 1:
            d, _, device = ring("x")[k]
            fanned(16 + d, f_x.at[h, x], device)
    copy_to("y6", partner, f_y.at[h, y], f_y.at[h, y])
    copy_to("z6", partner, f_z.at[h, z], f_z.at[h, z])
    copy_to("x6", partner, f_x.at[h, x], f_x.at[h, x])
    stages(0, K // PIVOTS)

    def fan_in(name, i, block):
        pltpu.make_async_copy(block, block, f_sems.at[1, i]).wait()
        copy_to(name, partner, block, block)

    for d in (1, 7, 2, 6, 3, 5, 4):
        fan_in("y6", d, f_y.at[h, lax.rem(y + NY - d, NY)])
        fan_in("z6", 8 + d, f_z.at[h, lax.rem(z + NZ - d, NZ)])
        if d in (7, 2, 6):
            e = {7: 1, 2: 3, 6: 2}[d]
            fan_in("x6", 16 + e, f_x.at[h, lax.rem(x + NX - e, NX)])

    def tiles(ref):
        rows = [jnp.concatenate([ref[2 * k], ref[2 * k + 1]], axis=1) for k in range(4)]
        return jnp.concatenate(rows, axis=0)

    def second_part(half):
        @pl.loop(0, NY)
        def _(i):
            parts = [tiles(f_y.at[half, i])]
            parts += [tiles(f_z.at[half, :, i])]
            parts += [f_x[half, q, i] for q in range(NX)]
            high, low = split2(jnp.concatenate(parts, axis=0))
            acc[...] += lax.dot_general(
                a_v[half, i], jnp.concatenate([high, low], axis=0), NT, preferred_element_type=f32
            )

    acc[...] = jnp.zeros_like(acc)
    second_part(h)
    arrived("y6", f_y.at[other])
    arrived("z6", f_z.at[other])
    arrived("x6", f_x.at[other])
    second_part(other)
    sec[...] = times_transposed(acc[:, :K] + acc[:, K:], work[:, K:])

    project(1, sec[...])
    gram_z(1)
    gram_x(1)
    two(1)
    gram_back(1)
    three(1)
    gram_done(1)
    stages(0, 2)
    gather = sums(1)
    e_y[z] = next(gather)
    spread("y7", "z", e_y.at[z])
    e_z[z] = next(gather)
    spread("z7", "z", e_z.at[z])
    e_x[x] = next(gather)
    spread("x7", "x", e_x.at[x])
    stages(2, K // PIVOTS)
    inverse = work[:, K:]
    basis[...] = times_transposed(sec[...], inverse) * scale_root
    arrived("y7", e_y.at[pl.ds(0, NZ - 1)])
    arrived("z7", e_z.at[pl.ds(0, NZ - 1)])
    arrived("x7", e_x.at[pl.ds(0, NX - 1)])
    summed = jnp.concatenate([tiles(e_y), tiles(e_z)] + [e_x[q] for q in range(NX)], axis=0)
    components[...] = times_transposed(summed.T, inverse) / scale_root

    for i, ref in pending:
        pltpu.make_async_copy(ref, ref, send_sems.at[i]).wait()
    for d in range(NY):
        pltpu.make_async_copy(mine, mine, s_send.at[8 + d]).wait()
    for d in NEAR:
        pltpu.make_async_copy(mine, mine, s_send.at[d]).wait()
    for d in FAR:
        quarter = s_v.at[h, y, pl.ds(0, QUARTER)]
        pltpu.make_async_copy(quarter, quarter, s_send.at[d]).wait()
        three_quarters = s_v.at[h, y, pl.ds(0, BLOCK - QUARTER)]
        pltpu.make_async_copy(three_quarters, three_quarters, q_send.at[d]).wait()
    for p in range(2):
        for j in range(NY // 2):
            pair = c_send.at[p, pl.ds(0, 2)]
            pltpu.make_async_copy(pair, pair, c_sems.at[p, 0, j]).wait()
    for d in range(1, NY):
        pltpu.make_async_copy(f_y.at[h, y], f_y.at[h, y], f_sems.at[0, d]).wait()
        pltpu.make_async_copy(f_z.at[h, z], f_z.at[h, z], f_sems.at[0, 8 + d]).wait()
    for d in range(1, NX):
        pltpu.make_async_copy(f_x.at[h, x], f_x.at[h, x], f_sems.at[0, 16 + d]).wait()


def on_device(activations, sketch):
    rows_total = activations.shape[0] * lax.axis_size("row") * lax.axis_size("col")
    vmem = pltpu.VMEM
    shapes = [
        vmem((ROWS, K), f32), vmem((2, NY, ROWS, BLOCK), bf16), vmem((2, NY, BLOCK, K), bf16), vmem((ROWS, K), f32),
        vmem((2 * K, ROWS), bf16), vmem((K, 2 * K), f32), vmem((ROWS, 2 * K), f32),
        vmem((2, 2 * NY, 8, K), f32), vmem((2, 2 * NY - 1, 8, K), f32),
        vmem((2, NZ, 8, K), f32), vmem((2, NX, 8, K), f32), vmem((2, 2 * NY, 8, K), f32),
        vmem((2, NY, K, BLOCK), bf16), vmem((2, NY, K, BLOCK), bf16),
        vmem((2, NY, 32, BLOCK), bf16), vmem((2, NZ, 64, K), bf16), vmem((2, NX, NY, 16, BLOCK), bf16),
        vmem((2, NY - 1, 32, BLOCK), bf16), vmem((2, NZ - 1, 64, K), bf16), vmem((2, NX - 1, NY, 16, BLOCK), bf16),
        vmem((2, NZ, 8, K), f32), vmem((2, NY, 8, K), f32), vmem((2, NY, 16, BLOCK), bf16),
        vmem((2, NZ - 1, 8, K), f32), vmem((2, NY - 1, 8, K), f32), vmem((2, NY - 1, 16, BLOCK), bf16),
        vmem((2, NX, 8, K), f32), vmem((2, NX, 8, K), f32), vmem((2, NZ, 16, BLOCK), f32),
        vmem((2, NY, NZ, 8, K), f32), vmem((2, NZ, NY, 8, K), f32), vmem((2, NX, NY, 16, BLOCK), f32),
        vmem((NZ, 8, K), f32), vmem((NZ, 8, K), f32), vmem((NX, 16, BLOCK), f32),
        pltpu.SemaphoreType.DMA((2,)), pltpu.SemaphoreType.DMA((16,)), pltpu.SemaphoreType.DMA((8,)),
        pltpu.SemaphoreType.DMA((8,)), pltpu.SemaphoreType.DMA((8,)), pltpu.SemaphoreType.DMA((8,)),
        pltpu.SemaphoreType.DMA((2, 2, NY // 2)), pltpu.SemaphoreType.DMA((2, 24)),
        pltpu.SemaphoreType.DMA((48,)), pltpu.SemaphoreType.DMA((48,)),
    ]
    here = pl.BlockSpec(memory_space=pltpu.VMEM)
    far = pl.BlockSpec(memory_space=pltpu.HBM)
    return pl.pallas_call(
        functools.partial(kernel, math.sqrt(rows_total)),
        out_shape=(jax.ShapeDtypeStruct((ROWS, K), f32), jax.ShapeDtypeStruct((BLOCK, K), f32)),
        in_specs=[far, far],
        out_specs=(here, here),
        scratch_shapes=shapes,
        compiler_params=pltpu.CompilerParams(
            collective_id=0, has_side_effects=True, vmem_limit_bytes=48 << 20
        ),
        name="subspace",
    )(activations, sketch)


def solution(mesh):
    placed = (P(("row", "col"), None), P("col", None))
    return jax.shard_map(
        on_device,
        mesh=mesh,
        in_specs=placed,
        out_specs=(P(("row", "col"), None), P("col", None)),
        check_vma=False,
    )
```

```python
import functools
import math

import jax
import jax.numpy as jnp
from jax import lax
from jax.experimental import pallas as pl
from jax.experimental.pallas import tpu as pltpu
from jax.sharding import PartitionSpec as P

f32, bf16 = jnp.float32, jnp.bfloat16
NX, NY, NZ = 4, 8, 8
K, BLOCK, ROWS = 128, 256, 512
PIVOTS = 16
QUARTER = BLOCK // NX
NT = (((1,), (1,)), ((), ()))
RING8 = (4, 3, 5, 2, 6, 1, 7)
RING4 = (2, 1, 3)
NEAR, FAR = (1, 7, 2, 6), (4, 3, 5)
COL16 = (8, 7, 9, 6, 10, 5, 11, 4, 12, 3, 13, 2, 14, 1, 15)


def split2(value):
    high = value.astype(bf16)
    return high, (value - high.astype(f32)).astype(bf16)


def split3(value):
    high = value.astype(bf16)
    rest = value - high.astype(f32)
    middle = rest.astype(bf16)
    return high, middle, (rest - middle.astype(f32)).astype(bf16)


def times_transposed(left, right):
    lh, ll = split2(left)
    rh, rl = split2(right)
    return lax.dot_general(
        jnp.concatenate([lh, ll, lh], axis=1),
        jnp.concatenate([rh, rh, rl], axis=1),
        NT,
        preferred_element_type=f32,
    )


def cholesky_stage(b, work):
    base = pl.multiple_of(b * PIVOTS, PIVOTS)
    panel = work[pl.ds(base, PIVOTS), :]
    g, w = panel[:, :K], panel[:, K:]
    shape = (PIVOTS, K)
    lane = lax.broadcasted_iota(jnp.int32, shape, 1)
    sub = lax.broadcasted_iota(jnp.int32, shape, 0)

    def column(k):
        return jnp.broadcast_to(jnp.sum(jnp.where(lane == base + k, g, 0.0), axis=1, keepdims=True), shape)

    def row(value, i):
        return jnp.broadcast_to(value[i : i + 1], shape)

    pivots = [column(k) for k in range(PIVOTS)]
    for i in range(PIVOTS):
        r = lax.rsqrt(row(pivots[i], i))
        low = jnp.where(sub > i, pivots[i] * r, 0.0)
        gi, wi = row(g, i) * r, row(w, i) * r
        g = jnp.where(sub == i, gi, g - low * gi)
        w = jnp.where(sub == i, wi, w - low * wi)
        for k in range(i + 1, PIVOTS):
            pivots[k] = pivots[k] - low * (row(pivots[k], i) * r)
    rows = jnp.concatenate([g, w], axis=1)
    work[pl.ds(base, PIVOTS), :] = rows
    left = split3(jnp.where(lane >= base + PIVOTS, g, 0.0))
    right = split3(rows)
    pairs = ((0, 0), (0, 1), (1, 0), (1, 1), (0, 2), (2, 0))
    work[...] -= lax.dot_general(
        jnp.concatenate([left[i] for i, _ in pairs], axis=0),
        jnp.concatenate([right[j] for _, j in pairs], axis=0),
        (((0,), (0,)), ((), ())),
        preferred_element_type=f32,
    )


def kernel(
    scale_root, a_hbm, s_hbm, basis, components,
    sec, a_v, s_v, f_acc, ft, work, coeffs,
    g_local, g_col, g_z, g_x, g_all,
    c_send, c_recv,
    y1s, z1s, x1s, y1r, z1r, x1r,
    y2s, z2s, x2s, v2s, w2s, y2r, z2r, x2r, v2r, w2r,
    y3, z3, x3, v3, w3, f_y, f_z, f_x, e_y, e_z, e_x,
    load_sem, s_send, s_recv, p_recv, q_send, q_recv, c_sems, f_sems, send_sems, recv_sems,
):
    row, col = lax.axis_index("row"), lax.axis_index("col")
    z, x, y, h = row // NX, lax.rem(row, NX), col // 2, lax.rem(col, 2)
    other = 1 - h

    def at(zz, xx, yy, hh):
        return (zz * NX + xx, yy * 2 + hh)

    def ring(axis):
        if axis == "y":
            return [(d, lax.rem(y + d, NY), at(z, x, lax.rem(y + d, NY), h)) for d in RING8]
        if axis == "col":
            spots = [lax.rem(col + d, 2 * NY) for d in COL16]
            return [(d, c, (row, c)) for d, c in zip(COL16, spots)]
        if axis == "z":
            return [(d, lax.rem(z + d, NZ), at(lax.rem(z + d, NZ), x, y, h)) for d in RING8]
        return [(d, lax.rem(x + d, NX), at(z, lax.rem(x + d, NX), y, h)) for d in RING4]

    partner = at(z, x, y, other)

    def columns(half, place):
        return a_v[half, :, pl.ds(pl.multiple_of(place * BLOCK, BLOCK), BLOCK)]

    pending = []
    slots = {}

    def slot(name):
        return slots.setdefault(name, len(slots))

    def copy_to(name, device, src, dst):
        i = slot(name)
        pltpu.make_async_remote_copy(
            src_ref=src, dst_ref=dst, send_sem=send_sems.at[i], recv_sem=recv_sems.at[i],
            device_id=device, device_id_type=pl.DeviceIdType.MESH,
        ).start()

    def arrived(name, ref):
        pltpu.make_async_copy(ref, ref, recv_sems.at[slot(name)]).wait()
        pending.append((slot(name), ref))

    def scatter(name, axis, src, dst):
        for d, place, device in ring(axis):
            copy_to(name, device, src.at[place], dst.at[d - 1])

    def spread(name, axis, ref):
        for _, _, device in ring(axis):
            copy_to(name, device, ref, ref)

    loads = [
        pltpu.make_async_copy(
            a_hbm.at[:, pl.ds((yy * 2 + hh) * BLOCK, BLOCK)], a_v.at[hh, :, pl.ds(yy * BLOCK, BLOCK)], load_sem.at[0]
        )
        for hh in range(2)
        for yy in range(NY)
    ]
    own_sketch = pltpu.make_async_copy(s_hbm, s_v.at[h, y], load_sem.at[1])
    own_sketch.start()
    for load in loads:
        load.start()
    barrier = pltpu.get_barrier_semaphore()
    peers = [device for axis in ("col", "z", "x") for _, _, device in ring(axis)]
    for device in peers:
        pl.semaphore_signal(barrier, inc=1, device_id=device, device_id_type=pl.DeviceIdType.MESH)
    own_sketch.wait()
    pl.semaphore_wait(barrier, len(peers))

    def sketch_copy(block, device, sends, recvs, d):
        return pltpu.make_async_remote_copy(
            src_ref=block, dst_ref=block, send_sem=sends, recv_sem=recvs.at[d],
            device_id=device, device_id_type=pl.DeviceIdType.MESH,
        )

    mine = s_v.at[h, y]
    span = pl.ds(pl.multiple_of(x * QUARTER, QUARTER), QUARTER)
    for d in FAR:
        sketch_copy(s_v.at[h, y, span], at(z, x, lax.rem(y + d, NY), h), s_send.at[d], q_recv, d).start()
    for d in NEAR:
        sketch_copy(mine, at(z, x, lax.rem(y + d, NY), h), s_send.at[d], s_recv, d).start()

    def hand_on(d, place):
        sketch_copy(s_v.at[h, place], partner, s_send.at[8 + d], p_recv, d).start()

    def origin(d):
        return lax.rem(y + NY - d, NY)

    def come(ds, size):
        for d in ds:
            part = s_v.at[h, origin(d), pl.ds(0, size)]
            pltpu.make_async_copy(part, part, s_recv.at[d]).wait()
            hand_on(d, origin(d))

    def add(half, ds):
        blocks = [(half, origin(d)) for d in ds]
        f_acc[...] += sum(jnp.dot(columns(*b), s_v[b], preferred_element_type=f32) for b in blocks)

    def add_other(ds):
        for d in ds:
            block = s_v.at[other, origin(d)]
            pltpu.make_async_copy(block, block, p_recv.at[d]).wait()
        add(other, ds)

    hand_on(0, y)
    pltpu.make_async_copy(a_v, a_v, load_sem.at[0]).wait()
    f_acc[...] = jnp.dot(columns(h, y), s_v[h, y], preferred_element_type=f32)
    come(NEAR[:2], BLOCK)
    for d in FAR:
        quarter = s_v.at[h, origin(d), span]
        pltpu.make_async_copy(quarter, quarter, q_recv.at[d]).wait()
        for _, _, device in ring("x"):
            sketch_copy(quarter, device, q_send.at[d], s_recv, d).start()
    come(NEAR[2:], BLOCK)
    add(h, NEAR)
    add_other((0,) + NEAR)
    come(FAR, BLOCK - QUARTER)
    add(h, FAR)
    add_other(FAR)

    def project(p, tall):
        high, low = split2(tall.T)
        ft[:K, :] = high
        ft[K:, :] = low

        def gram_first():
            both = ft[...]
            square = lax.dot_general(both, both, NT, preferred_element_type=f32)
            gram = (square[:K, :K] + square[K:, K:]) + (square[:K, K:] + square[K:, :K])
            g_local[p] = gram.reshape(2 * NY, 8, K)
            scatter(f"gc{p}", "col", g_local.at[p], g_col.at[p])

        if p == 1:
            gram_first()

        @pl.loop(0, NY // 2)
        def _(j):
            for i in (2 * j, 2 * j + 1):
                both = jnp.dot(ft[...], columns(other, i), preferred_element_type=f32)
                c_send[p, i] = (both[:K] + both[K:]).astype(bf16)
            pair = pl.ds(2 * j, 2)
            pltpu.make_async_remote_copy(
                src_ref=c_send.at[p, pair], dst_ref=c_recv.at[p, pair],
                send_sem=c_sems.at[p, 0, j], recv_sem=c_sems.at[p, 1, j],
                device_id=partner, device_id_type=pl.DeviceIdType.MESH,
            ).start()

        if p == 0:
            gram_first()

        @pl.loop(0, NY // 2)
        def _(j):
            values = []
            for i in (2 * j, 2 * j + 1):
                both = jnp.dot(ft[...], columns(h, i), preferred_element_type=f32)
                values.append(both[:K] + both[K:])
            pair = c_recv.at[p, pl.ds(2 * j, 2)]
            pltpu.make_async_copy(pair, pair, c_sems.at[p, 1, j]).wait()
            values = [value + pair[i].astype(f32) for i, value in enumerate(values)]
            for place, value in zip((2 * j, 2 * j + 1), values):
                y1s[p, place] = value[:32].astype(bf16)
                for q in range(NX):
                    both = [value[r + 8 * q : r + 8 * q + 8] for r in (64, 96)]
                    x1s[p, q, place] = jnp.concatenate(both, axis=0).astype(bf16)
            for q in range(NZ):
                r, c = 32 + 8 * (q // 2), K * (q % 2)
                both = jnp.concatenate([value[r : r + 8, c : c + K] for value in values], axis=0)
                z1s[p, q, pl.ds(pl.multiple_of(j * 16, 16), 16)] = both.astype(bf16)

        scatter(f"x1{p}", "x", x1s.at[p], x1r.at[p])
        scatter(f"y1{p}", "y", y1s.at[p], y1r.at[p])
        scatter(f"z1{p}", "z", z1s.at[p], z1r.at[p])

    def gram_z(p):
        arrived(f"gc{p}", g_col.at[p])
        g_z[p, z] = g_local[p, col] + jnp.sum(g_col[p], axis=0)
        spread(f"gz{p}", "z", g_z.at[p, z])

    def gram_x(p):
        arrived(f"gz{p}", g_z.at[p, pl.ds(0, NZ - 1)])
        g_x[p, x] = jnp.sum(g_z[p], axis=0)
        spread(f"gx{p}", "x", g_x.at[p, x])

    def gram_back(p):
        arrived(f"gx{p}", g_x.at[p, pl.ds(0, NX - 1)])
        g_all[p, col] = jnp.sum(g_x[p], axis=0)
        spread(f"ga{p}", "col", g_all.at[p, col])

    def gram_done(p):
        arrived(f"ga{p}", g_all.at[p, pl.ds(0, 2 * NY - 1)])
        ri = lax.broadcasted_iota(jnp.int32, (K, K), 0)
        ci = lax.broadcasted_iota(jnp.int32, (K, K), 1)
        work[:, :K] = g_all[p].reshape(K, K)
        work[:, K:] = jnp.where(ri == ci, 1.0, 0.0)

    def stages(lo, hi):
        @pl.loop(lo, hi)
        def _(b):
            cholesky_stage(b, work)

    def total(own, parts):
        return own.astype(f32) + jnp.sum(parts.astype(f32), axis=0)

    def two(p):
        arrived(f"x1{p}", x1r.at[p])
        value = total(x1s[p, x], x1r[p])
        if p == 0:
            v2s[...] = value[:, :8]
            scatter("v2", "y", v2s, v2r)
            w2s[...] = value[:, 8:]
            scatter("w2", "z", w2s, w2r)
        else:
            x2s[...] = value.astype(bf16)
            scatter("x2", "y", x2s, x2r)
        arrived(f"y1{p}", y1r.at[p])
        value = total(y1s[p, y], y1r[p])
        for q in range(NZ):
            y2s[p, q] = value[8 * (q // 2) : 8 * (q // 2) + 8, K * (q % 2) : K * (q % 2) + K]
        scatter(f"y2{p}", "z", y2s.at[p], y2r.at[p])
        arrived(f"z1{p}", z1r.at[p])
        z2s[p] = total(z1s[p, z], z1r[p]).reshape(NY, 8, K)
        scatter(f"z2{p}", "y", z2s.at[p], z2r.at[p])

    def three(p):
        arrived(f"y2{p}", y2r.at[p])
        y3[p, x] = total(y2s[p, z], y2r[p])
        spread(f"y3{p}", "x", y3.at[p, x])
        arrived(f"z2{p}", z2r.at[p])
        z3[p, x] = total(z2s[p, y], z2r[p])
        spread(f"z3{p}", "x", z3.at[p, x])
        if p == 0:
            arrived("v2", v2r)
            v3[z] = total(v2s[y], v2r[...])
            spread("v3", "z", v3.at[z])
            arrived("w2", w2r)
            w3[y] = total(w2s[z], w2r[...])
            spread("w3", "y", w3.at[y])
        else:
            arrived("x2", x2r)
            x3[z] = total(x2s[y], x2r[...])
            spread("x3", "z", x3.at[z])

    def sums(p):
        arrived(f"y3{p}", y3.at[p, pl.ds(0, NX - 1)])
        yield jnp.sum(y3[p], axis=0)
        arrived(f"z3{p}", z3.at[p, pl.ds(0, NX - 1)])
        yield jnp.sum(z3[p], axis=0)
        for name, ref in (("v3", v3), ("w3", w3)) if p == 0 else (("x3", x3),):
            arrived(name, ref.at[pl.ds(0, NZ - 1)])
            yield jnp.sum(ref[...], axis=0)

    project(0, f_acc[...])
    gram_z(0)
    two(0)
    gram_x(0)
    three(0)
    gram_back(0)
    gather = sums(0)
    f_y[h, y, z] = next(gather)
    spread("y4", "z", f_y.at[h, y, z])
    f_z[h, z, y] = next(gather)
    spread("z4", "y", f_z.at[h, z, y])
    f_x[h, x, 0, y] = next(gather)
    spread("v4", "y", f_x.at[h, x, 0, y])
    f_x[h, x, 1, z] = next(gather)
    spread("w4", "z", f_x.at[h, x, 1, z])
    gram_done(0)
    arrived("y4", f_y.at[h, y, pl.ds(0, NZ - 1)])
    arrived("z4", f_z.at[h, z, pl.ds(0, NY - 1)])
    arrived("v4", f_x.at[h, x, 0, pl.ds(0, NY - 1)])
    arrived("w4", f_x.at[h, x, 1, pl.ds(0, NZ - 1)])

    def fanned(i, block, device):
        pltpu.make_async_remote_copy(
            src_ref=block, dst_ref=block, send_sem=f_sems.at[0, i], recv_sem=f_sems.at[1, i],
            device_id=device, device_id_type=pl.DeviceIdType.MESH,
        ).start()

    for k, (d, _, device) in enumerate(ring("y")):
        fanned(d, f_y.at[h, y], device)
        fanned(8 + d, f_z.at[h, z], ring("z")[k][2])
        if k < NX - 1:
            d, _, device = ring("x")[k]
            fanned(16 + d, f_x.at[h, x], device)
    copy_to("y6", partner, f_y.at[h, y], f_y.at[h, y])
    copy_to("z6", partner, f_z.at[h, z], f_z.at[h, z])
    copy_to("x6", partner, f_x.at[h, x], f_x.at[h, x])
    stages(0, K // PIVOTS)

    def fan_in(name, i, block):
        pltpu.make_async_copy(block, block, f_sems.at[1, i]).wait()
        copy_to(name, partner, block, block)

    for d in (1, 7, 2, 6, 3, 5, 4):
        fan_in("y6", d, f_y.at[h, lax.rem(y + NY - d, NY)])
        fan_in("z6", 8 + d, f_z.at[h, lax.rem(z + NZ - d, NZ)])
        if d in (7, 2, 6):
            e = {7: 1, 2: 3, 6: 2}[d]
            fan_in("x6", 16 + e, f_x.at[h, lax.rem(x + NX - e, NX)])

    def tiles(ref):
        rows = [jnp.concatenate([ref[2 * k], ref[2 * k + 1]], axis=1) for k in range(4)]
        return jnp.concatenate(rows, axis=0)

    def second_part(half):
        @pl.loop(0, NY)
        def _(i):
            parts = [tiles(f_y.at[half, i]), tiles(f_z.at[half, :, i])]
            parts += [f_x[half, q, k, i] for k in range(2) for q in range(NX)]
            high, low = split2(jnp.concatenate(parts, axis=0))
            span = pl.ds(pl.multiple_of(i * BLOCK, BLOCK), BLOCK)
            coeffs[half, :, span] = jnp.concatenate([high, low], axis=0)

        both = lax.dot_general(a_v[half], coeffs[half], NT, preferred_element_type=f32)
        return both[:, :K] + both[:, K:]

    f_acc[...] = second_part(h)
    arrived("y6", f_y.at[other])
    arrived("z6", f_z.at[other])
    arrived("x6", f_x.at[other])
    sec[...] = times_transposed(f_acc[...] + second_part(other), work[:, K:])

    project(1, sec[...])
    gram_z(1)
    gram_x(1)
    two(1)
    gram_back(1)
    three(1)
    gram_done(1)
    stages(0, 2)
    gather = sums(1)
    e_y[z] = next(gather)
    spread("y7", "z", e_y.at[z])
    e_z[z] = next(gather)
    spread("z7", "z", e_z.at[z])
    e_x[x] = next(gather)
    spread("x7", "x", e_x.at[x])
    stages(2, K // PIVOTS)
    inverse = work[:, K:]
    basis[...] = times_transposed(sec[...], inverse) * scale_root
    arrived("y7", e_y.at[pl.ds(0, NZ - 1)])
    arrived("z7", e_z.at[pl.ds(0, NZ - 1)])
    arrived("x7", e_x.at[pl.ds(0, NX - 1)])
    summed = jnp.concatenate([tiles(e_y), tiles(e_z)] + [e_x[q, k : k + 8] for k in (0, 8) for q in range(NX)], axis=0)
    components[...] = times_transposed(summed.T, inverse) / scale_root

    for i, ref in pending:
        pltpu.make_async_copy(ref, ref, send_sems.at[i]).wait()
    for d in range(NY):
        pltpu.make_async_copy(mine, mine, s_send.at[8 + d]).wait()
    for d in NEAR:
        pltpu.make_async_copy(mine, mine, s_send.at[d]).wait()
    for d in FAR:
        quarter = s_v.at[h, y, pl.ds(0, QUARTER)]
        pltpu.make_async_copy(quarter, quarter, s_send.at[d]).wait()
        three_quarters = s_v.at[h, y, pl.ds(0, BLOCK - QUARTER)]
        pltpu.make_async_copy(three_quarters, three_quarters, q_send.at[d]).wait()
    for p in range(2):
        for j in range(NY // 2):
            pair = c_send.at[p, pl.ds(0, 2)]
            pltpu.make_async_copy(pair, pair, c_sems.at[p, 0, j]).wait()
    for d in range(1, NY):
        pltpu.make_async_copy(f_y.at[h, y], f_y.at[h, y], f_sems.at[0, d]).wait()
        pltpu.make_async_copy(f_z.at[h, z], f_z.at[h, z], f_sems.at[0, 8 + d]).wait()
    for d in range(1, NX):
        pltpu.make_async_copy(f_x.at[h, x], f_x.at[h, x], f_sems.at[0, 16 + d]).wait()


def on_device(activations, sketch):
    rows_total = activations.shape[0] * lax.axis_size("row") * lax.axis_size("col")
    vmem = pltpu.VMEM
    shapes = [
        vmem((ROWS, K), f32), vmem((2, ROWS, NY * BLOCK), bf16), vmem((2, NY, BLOCK, K), bf16), vmem((ROWS, K), f32),
        vmem((2 * K, ROWS), bf16), vmem((K, 2 * K), f32), vmem((2, 2 * K, NY * BLOCK), bf16),
        vmem((2, 2 * NY, 8, K), f32), vmem((2, 2 * NY - 1, 8, K), f32),
        vmem((2, NZ, 8, K), f32), vmem((2, NX, 8, K), f32), vmem((2, 2 * NY, 8, K), f32),
        vmem((2, NY, K, BLOCK), bf16), vmem((2, NY, K, BLOCK), bf16),
        vmem((2, NY, 32, BLOCK), bf16), vmem((2, NZ, 64, K), bf16), vmem((2, NX, NY, 16, BLOCK), bf16),
        vmem((2, NY - 1, 32, BLOCK), bf16), vmem((2, NZ - 1, 64, K), bf16), vmem((2, NX - 1, NY, 16, BLOCK), bf16),
        vmem((2, NZ, 8, K), f32), vmem((2, NY, 8, K), f32), vmem((NY, 16, BLOCK), bf16),
        vmem((NY, 8, BLOCK), f32), vmem((NZ, 8, BLOCK), f32),
        vmem((2, NZ - 1, 8, K), f32), vmem((2, NY - 1, 8, K), f32), vmem((NY - 1, 16, BLOCK), bf16),
        vmem((NY - 1, 8, BLOCK), f32), vmem((NZ - 1, 8, BLOCK), f32),
        vmem((2, NX, 8, K), f32), vmem((2, NX, 8, K), f32), vmem((NZ, 16, BLOCK), f32),
        vmem((NZ, 8, BLOCK), f32), vmem((NY, 8, BLOCK), f32),
        vmem((2, NY, NZ, 8, K), f32), vmem((2, NZ, NY, 8, K), f32), vmem((2, NX, 2, NY, 8, BLOCK), f32),
        vmem((NZ, 8, K), f32), vmem((NZ, 8, K), f32), vmem((NX, 16, BLOCK), f32),
        pltpu.SemaphoreType.DMA((2,)), pltpu.SemaphoreType.DMA((16,)), pltpu.SemaphoreType.DMA((8,)),
        pltpu.SemaphoreType.DMA((8,)), pltpu.SemaphoreType.DMA((8,)), pltpu.SemaphoreType.DMA((8,)),
        pltpu.SemaphoreType.DMA((2, 2, NY // 2)), pltpu.SemaphoreType.DMA((2, 24)),
        pltpu.SemaphoreType.DMA((48,)), pltpu.SemaphoreType.DMA((48,)),
    ]
    here = pl.BlockSpec(memory_space=pltpu.VMEM)
    far = pl.BlockSpec(memory_space=pltpu.HBM)
    return pl.pallas_call(
        functools.partial(kernel, math.sqrt(rows_total)),
        out_shape=(jax.ShapeDtypeStruct((ROWS, K), f32), jax.ShapeDtypeStruct((BLOCK, K), f32)),
        in_specs=[far, far],
        out_specs=(here, here),
        scratch_shapes=shapes,
        compiler_params=pltpu.CompilerParams(
            collective_id=0, has_side_effects=True, vmem_limit_bytes=52 << 20
        ),
        name="subspace",
    )(activations, sketch)


def solution(mesh):
    placed = (P(("row", "col"), None), P("col", None))
    return jax.shard_map(
        on_device,
        mesh=mesh,
        in_specs=placed,
        out_specs=(P(("row", "col"), None), P("col", None)),
        check_vma=False,
    )
```

```python
import functools
import math

import jax
import jax.numpy as jnp
from jax import lax
from jax.experimental import pallas as pl
from jax.experimental.pallas import tpu as pltpu
from jax.sharding import PartitionSpec as P

f32, bf16 = jnp.float32, jnp.bfloat16
NX, NY, NZ = 4, 8, 8
K, BLOCK, ROWS = 128, 256, 512
PIVOTS = 16
QUARTER = BLOCK // NX
NT = (((1,), (1,)), ((), ()))
RING8 = (4, 3, 5, 2, 6, 1, 7)
RING4 = (2, 1, 3)
NEAR, FAR = (1, 7, 2, 6), (4, 3, 5)
COL16 = (8, 7, 9, 6, 10, 5, 11, 4, 12, 3, 13, 2, 14, 1, 15)


def split2(value):
    high = value.astype(bf16)
    return high, (value - high.astype(f32)).astype(bf16)


def split3(value):
    high = value.astype(bf16)
    rest = value - high.astype(f32)
    middle = rest.astype(bf16)
    return high, middle, (rest - middle.astype(f32)).astype(bf16)


def times_transposed(left, right):
    lh, ll = split2(left)
    rh, rl = split2(right)
    return lax.dot_general(
        jnp.concatenate([lh, ll, lh], axis=1),
        jnp.concatenate([rh, rh, rl], axis=1),
        NT,
        preferred_element_type=f32,
    )


def cholesky_stage(b, work):
    base = pl.multiple_of(b * PIVOTS, PIVOTS)
    panel = work[pl.ds(base, PIVOTS), :]
    g, w = panel[:, :K], panel[:, K:]
    shape = (PIVOTS, K)
    lane = lax.broadcasted_iota(jnp.int32, shape, 1)
    sub = lax.broadcasted_iota(jnp.int32, shape, 0)

    def column(k):
        return jnp.broadcast_to(jnp.sum(jnp.where(lane == base + k, g, 0.0), axis=1, keepdims=True), shape)

    def row(value, i):
        return jnp.broadcast_to(value[i : i + 1], shape)

    pivots = [column(k) for k in range(PIVOTS)]
    for i in range(PIVOTS):
        r = lax.rsqrt(row(pivots[i], i))
        low = jnp.where(sub > i, pivots[i] * r, 0.0)
        gi, wi = row(g, i) * r, row(w, i) * r
        g = jnp.where(sub == i, gi, g - low * gi)
        w = jnp.where(sub == i, wi, w - low * wi)
        for k in range(i + 1, PIVOTS):
            pivots[k] = pivots[k] - low * (row(pivots[k], i) * r)
    rows = jnp.concatenate([g, w], axis=1)
    work[pl.ds(base, PIVOTS), :] = rows
    left = split3(jnp.where(lane >= base + PIVOTS, g, 0.0))
    right = split3(rows)
    pairs = ((0, 0), (0, 1), (1, 0), (1, 1), (0, 2), (2, 0))
    work[...] -= lax.dot_general(
        jnp.concatenate([left[i] for i, _ in pairs], axis=0),
        jnp.concatenate([right[j] for _, j in pairs], axis=0),
        (((0,), (0,)), ((), ())),
        preferred_element_type=f32,
    )


def kernel(
    scale_root, a_hbm, s_hbm, basis, components,
    sec, a_v, s_v, f_acc, ft, work, coeffs,
    g_local, g_col, g_z, g_x, g_all,
    c_send, c_recv,
    y1s, z1s, x1s, y1r, z1r, x1r,
    over_y, over_z, over_y_in, over_z_in, y2s, z2s, x2s, y2r, z2r, x2r,
    yz3, v3, w3, y_full, z_full, y3, z3, x3, f_y, f_z, f_x, e_y, e_z, e_x,
    load_sem, s_send, s_recv, p_recv, q_send, q_recv, c_sems, f_sems, send_sems, recv_sems,
):
    row, col = lax.axis_index("row"), lax.axis_index("col")
    z, x, y, h = row // NX, lax.rem(row, NX), col // 2, lax.rem(col, 2)
    other = 1 - h

    def at(zz, xx, yy, hh):
        return (zz * NX + xx, yy * 2 + hh)

    def ring(axis):
        if axis == "y":
            return [(d, lax.rem(y + d, NY), at(z, x, lax.rem(y + d, NY), h)) for d in RING8]
        if axis == "col":
            spots = [lax.rem(col + d, 2 * NY) for d in COL16]
            return [(d, c, (row, c)) for d, c in zip(COL16, spots)]
        if axis == "z":
            return [(d, lax.rem(z + d, NZ), at(lax.rem(z + d, NZ), x, y, h)) for d in RING8]
        return [(d, lax.rem(x + d, NX), at(z, lax.rem(x + d, NX), y, h)) for d in RING4]

    partner = at(z, x, y, other)

    def columns(half, place):
        return a_v[half, :, pl.ds(pl.multiple_of(place * BLOCK, BLOCK), BLOCK)]

    pending = []
    slots = {}

    def slot(name):
        return slots.setdefault(name, len(slots))

    def copy_to(name, device, src, dst):
        i = slot(name)
        pltpu.make_async_remote_copy(
            src_ref=src, dst_ref=dst, send_sem=send_sems.at[i], recv_sem=recv_sems.at[i],
            device_id=device, device_id_type=pl.DeviceIdType.MESH,
        ).start()

    def arrived(name, ref):
        pltpu.make_async_copy(ref, ref, recv_sems.at[slot(name)]).wait()
        pending.append((slot(name), ref))

    def scatter(name, axis, src, dst):
        for d, place, device in ring(axis):
            copy_to(name, device, src.at[place], dst.at[d - 1])

    def spread(name, axis, ref):
        for _, _, device in ring(axis):
            copy_to(name, device, ref, ref)

    loads = [
        pltpu.make_async_copy(
            a_hbm.at[:, pl.ds((yy * 2 + hh) * BLOCK, BLOCK)], a_v.at[hh, :, pl.ds(yy * BLOCK, BLOCK)], load_sem.at[0]
        )
        for hh in range(2)
        for yy in range(NY)
    ]
    own_sketch = pltpu.make_async_copy(s_hbm, s_v.at[h, y], load_sem.at[1])
    own_sketch.start()
    for load in loads:
        load.start()
    barrier = pltpu.get_barrier_semaphore()
    peers = [device for axis in ("col", "z", "x") for _, _, device in ring(axis)]
    for device in peers:
        pl.semaphore_signal(barrier, inc=1, device_id=device, device_id_type=pl.DeviceIdType.MESH)
    own_sketch.wait()
    pl.semaphore_wait(barrier, len(peers))

    def sketch_copy(block, device, sends, recvs, d):
        return pltpu.make_async_remote_copy(
            src_ref=block, dst_ref=block, send_sem=sends, recv_sem=recvs.at[d],
            device_id=device, device_id_type=pl.DeviceIdType.MESH,
        )

    mine = s_v.at[h, y]
    span = pl.ds(pl.multiple_of(x * QUARTER, QUARTER), QUARTER)
    for d in FAR:
        sketch_copy(s_v.at[h, y, span], at(z, x, lax.rem(y + d, NY), h), s_send.at[d], q_recv, d).start()
    for d in NEAR:
        sketch_copy(mine, at(z, x, lax.rem(y + d, NY), h), s_send.at[d], s_recv, d).start()

    def hand_on(d, place):
        sketch_copy(s_v.at[h, place], partner, s_send.at[8 + d], p_recv, d).start()

    def origin(d):
        return lax.rem(y + NY - d, NY)

    def come(ds, size):
        for d in ds:
            part = s_v.at[h, origin(d), pl.ds(0, size)]
            pltpu.make_async_copy(part, part, s_recv.at[d]).wait()
            hand_on(d, origin(d))

    def add(half, ds):
        blocks = [(half, origin(d)) for d in ds]
        f_acc[...] += sum(jnp.dot(columns(*b), s_v[b], preferred_element_type=f32) for b in blocks)

    def add_other(ds):
        for d in ds:
            block = s_v.at[other, origin(d)]
            pltpu.make_async_copy(block, block, p_recv.at[d]).wait()
        add(other, ds)

    hand_on(0, y)
    pltpu.make_async_copy(a_v, a_v, load_sem.at[0]).wait()
    f_acc[...] = jnp.dot(columns(h, y), s_v[h, y], preferred_element_type=f32)
    come(NEAR[:2], BLOCK)
    for d in FAR:
        quarter = s_v.at[h, origin(d), span]
        pltpu.make_async_copy(quarter, quarter, q_recv.at[d]).wait()
        for _, _, device in ring("x"):
            sketch_copy(quarter, device, q_send.at[d], s_recv, d).start()
    come(NEAR[2:], BLOCK)
    add(h, NEAR)
    add_other((0,) + NEAR)
    come(FAR, BLOCK - QUARTER)
    add(h, FAR)
    add_other(FAR)

    def project(p, tall):
        high, low = split2(tall.T)
        ft[:K, :] = high
        ft[K:, :] = low

        def gram_first():
            both = ft[...]
            square = lax.dot_general(both, both, NT, preferred_element_type=f32)
            gram = (square[:K, :K] + square[K:, K:]) + (square[:K, K:] + square[K:, :K])
            g_local[p] = gram.reshape(2 * NY, 8, K)
            scatter(f"gc{p}", "col", g_local.at[p], g_col.at[p])

        if p == 1:
            gram_first()

        @pl.loop(0, NY // 2)
        def _(j):
            for i in (2 * j, 2 * j + 1):
                both = jnp.dot(ft[...], columns(other, i), preferred_element_type=f32)
                c_send[p, i] = (both[:K] + both[K:]).astype(bf16)
            pair = pl.ds(2 * j, 2)
            pltpu.make_async_remote_copy(
                src_ref=c_send.at[p, pair], dst_ref=c_recv.at[p, pair],
                send_sem=c_sems.at[p, 0, j], recv_sem=c_sems.at[p, 1, j],
                device_id=partner, device_id_type=pl.DeviceIdType.MESH,
            ).start()

        @pl.loop(0, NY // 2)
        def _(j):
            values = []
            for i in (2 * j, 2 * j + 1):
                both = jnp.dot(ft[...], columns(h, i), preferred_element_type=f32)
                values.append(both[:K] + both[K:])
            pair = c_recv.at[p, pl.ds(2 * j, 2)]
            pltpu.make_async_copy(pair, pair, c_sems.at[p, 1, j]).wait()
            values = [value + pair[i].astype(f32) for i, value in enumerate(values)]
            for place, value in zip((2 * j, 2 * j + 1), values):
                y1s[p, place] = value[:32].astype(bf16)
                for q in range(NX):
                    both = [value[r + 8 * q : r + 8 * q + 8] for r in (64, 96)]
                    x1s[p, q, place] = jnp.concatenate(both, axis=0).astype(bf16)
            for q in range(NZ):
                r, c = 32 + 8 * (q // 2), K * (q % 2)
                both = jnp.concatenate([value[r : r + 8, c : c + K] for value in values], axis=0)
                z1s[p, q, pl.ds(pl.multiple_of(j * 16, 16), 16)] = both.astype(bf16)

        scatter(f"x1{p}", "x", x1s.at[p], x1r.at[p])
        scatter(f"y1{p}", "y", y1s.at[p], y1r.at[p])
        scatter(f"z1{p}", "z", z1s.at[p], z1r.at[p])
        if p == 0:
            gram_first()

    def gram_z(p):
        arrived(f"gc{p}", g_col.at[p])
        g_z[p, z] = g_local[p, col] + jnp.sum(g_col[p], axis=0)
        spread(f"gz{p}", "z", g_z.at[p, z])

    def gram_x(p):
        arrived(f"gz{p}", g_z.at[p, pl.ds(0, NZ - 1)])
        g_x[p, x] = jnp.sum(g_z[p], axis=0)
        spread(f"gx{p}", "x", g_x.at[p, x])

    def gram_back(p):
        arrived(f"gx{p}", g_x.at[p, pl.ds(0, NX - 1)])
        g_all[p, col] = jnp.sum(g_x[p], axis=0)
        spread(f"ga{p}", "col", g_all.at[p, col])

    def gram_done(p):
        arrived(f"ga{p}", g_all.at[p, pl.ds(0, 2 * NY - 1)])
        ri = lax.broadcasted_iota(jnp.int32, (K, K), 0)
        ci = lax.broadcasted_iota(jnp.int32, (K, K), 1)
        work[:, :K] = g_all[p].reshape(K, K)
        work[:, K:] = jnp.where(ri == ci, 1.0, 0.0)

    def stages(lo, hi):
        @pl.loop(lo, hi)
        def _(b):
            cholesky_stage(b, work)

    def total(own, parts):
        return own.astype(f32) + jnp.sum(parts.astype(f32), axis=0)

    def y_tiles(p):
        arrived(f"y1{p}", y1r.at[p])
        value = total(y1s[p, y], y1r[p])
        return [value[8 * (q // 2) : 8 * (q // 2) + 8, K * (q % 2) : K * (q % 2) + K] for q in range(NZ)]

    def z_tiles(p):
        arrived(f"z1{p}", z1r.at[p])
        return total(z1s[p, z], z1r[p]).reshape(NY, 8, K)

    def two_first():
        arrived("x10", x1r.at[0])
        value = total(x1s[0, x], x1r[0])
        for q, tile in enumerate(y_tiles(0)):
            over_z[q, :, :K] = tile
            over_z[q, :, K:] = value[q, 8:]
        scatter("wz", "z", over_z, over_z_in)
        over_y[:, :, :K] = z_tiles(0)
        over_y[:, :, K:] = value[:, :8]
        scatter("wy", "y", over_y, over_y_in)

    def three_first():
        arrived("wz", over_z_in)
        value = total(over_z[z], over_z_in[...])
        yz3[x, :, :K] = value[:, :K]
        w3[y] = value[:, K:]
        spread("w3", "y", w3.at[y])
        arrived("wy", over_y_in)
        value = total(over_y[y], over_y_in[...])
        yz3[x, :, K:] = value[:, :K]
        v3[z] = value[:, K:]
        spread("v3", "z", v3.at[z])
        spread("yz3", "x", yz3.at[x])

    def four_first():
        arrived("yz3", yz3.at[pl.ds(0, NX - 1)])
        value = jnp.sum(yz3[...], axis=0)
        arrived("w3", w3.at[pl.ds(0, NY - 1)])
        z_full[z, :, :K] = value[:, :K]
        z_full[z, :, K:] = jnp.sum(w3[...], axis=0)
        spread("z4", "z", z_full.at[z])
        arrived("v3", v3.at[pl.ds(0, NZ - 1)])
        y_full[y, :, :K] = value[:, K:]
        y_full[y, :, K:] = jnp.sum(v3[...], axis=0)
        spread("y4", "y", y_full.at[y])

    def two():
        arrived("x11", x1r.at[1])
        x2s[...] = total(x1s[1, x], x1r[1]).astype(bf16)
        scatter("x2", "y", x2s, x2r)
        for q, tile in enumerate(y_tiles(1)):
            y2s[q] = tile
        scatter("y2", "z", y2s, y2r)
        z2s[...] = z_tiles(1)
        scatter("z2", "y", z2s, z2r)

    def three():
        arrived("y2", y2r)
        y3[x] = total(y2s[z], y2r[...])
        spread("y3", "x", y3.at[x])
        arrived("z2", z2r)
        z3[x] = total(z2s[y], z2r[...])
        spread("z3", "x", z3.at[x])
        arrived("x2", x2r)
        x3[z] = total(x2s[y], x2r[...])
        spread("x3", "z", x3.at[z])

    project(0, f_acc[...])
    gram_z(0)
    two_first()
    gram_x(0)
    three_first()
    gram_back(0)
    four_first()
    arrived("z4", z_full.at[pl.ds(0, NZ - 1)])
    f_y[h, y] = z_full[:, :, :K]
    f_x[h, x, 1] = z_full[:, :, K:]
    arrived("y4", y_full.at[pl.ds(0, NY - 1)])
    f_z[h, z] = y_full[:, :, :K]
    f_x[h, x, 0] = y_full[:, :, K:]

    def fanned(i, block, device):
        pltpu.make_async_remote_copy(
            src_ref=block, dst_ref=block, send_sem=f_sems.at[0, i], recv_sem=f_sems.at[1, i],
            device_id=device, device_id_type=pl.DeviceIdType.MESH,
        ).start()

    for k, (d, _, device) in enumerate(ring("y")):
        fanned(d, f_y.at[h, y], device)
        fanned(8 + d, f_z.at[h, z], ring("z")[k][2])
        if k < NX - 1:
            d, _, device = ring("x")[k]
            fanned(16 + d, f_x.at[h, x], device)
    copy_to("y6", partner, f_y.at[h, y], f_y.at[h, y])
    copy_to("z6", partner, f_z.at[h, z], f_z.at[h, z])
    copy_to("x6", partner, f_x.at[h, x], f_x.at[h, x])
    gram_done(0)
    stages(0, K // PIVOTS)

    def fan_in(name, i, block):
        pltpu.make_async_copy(block, block, f_sems.at[1, i]).wait()
        copy_to(name, partner, block, block)

    for d in (1, 7, 2, 6, 3, 5, 4):
        fan_in("y6", d, f_y.at[h, lax.rem(y + NY - d, NY)])
        fan_in("z6", 8 + d, f_z.at[h, lax.rem(z + NZ - d, NZ)])
        if d in (7, 2, 6):
            e = {7: 1, 2: 3, 6: 2}[d]
            fan_in("x6", 16 + e, f_x.at[h, lax.rem(x + NX - e, NX)])

    def tiles(ref):
        rows = [jnp.concatenate([ref[2 * k], ref[2 * k + 1]], axis=1) for k in range(4)]
        return jnp.concatenate(rows, axis=0)

    def second_part(half):
        @pl.loop(0, NY)
        def _(i):
            parts = [tiles(f_y.at[half, i]), tiles(f_z.at[half, :, i])]
            parts += [f_x[half, q, k, i] for k in range(2) for q in range(NX)]
            high, low = split2(jnp.concatenate(parts, axis=0))
            span = pl.ds(pl.multiple_of(i * BLOCK, BLOCK), BLOCK)
            coeffs[half, :, span] = jnp.concatenate([high, low], axis=0)

        both = lax.dot_general(a_v[half], coeffs[half], NT, preferred_element_type=f32)
        return both[:, :K] + both[:, K:]

    f_acc[...] = second_part(h)
    arrived("y6", f_y.at[other])
    arrived("z6", f_z.at[other])
    arrived("x6", f_x.at[other])
    sec[...] = times_transposed(f_acc[...] + second_part(other), work[:, K:])

    project(1, sec[...])
    gram_z(1)
    gram_x(1)
    two()
    gram_back(1)
    three()
    arrived("y3", y3.at[pl.ds(0, NX - 1)])
    e_y[z] = jnp.sum(y3[...], axis=0)
    spread("y7", "z", e_y.at[z])
    arrived("z3", z3.at[pl.ds(0, NX - 1)])
    e_z[z] = jnp.sum(z3[...], axis=0)
    spread("z7", "z", e_z.at[z])
    gram_done(1)
    stages(0, 3)
    arrived("x3", x3.at[pl.ds(0, NZ - 1)])
    e_x[x] = jnp.sum(x3[...], axis=0)
    spread("x7", "x", e_x.at[x])
    stages(3, K // PIVOTS)
    inverse = work[:, K:]
    basis[...] = times_transposed(sec[...], inverse) * scale_root
    arrived("y7", e_y.at[pl.ds(0, NZ - 1)])
    arrived("z7", e_z.at[pl.ds(0, NZ - 1)])
    arrived("x7", e_x.at[pl.ds(0, NX - 1)])
    summed = jnp.concatenate([tiles(e_y), tiles(e_z)] + [e_x[q, k : k + 8] for k in (0, 8) for q in range(NX)], axis=0)
    components[...] = times_transposed(summed.T, inverse) / scale_root

    for i, ref in pending:
        pltpu.make_async_copy(ref, ref, send_sems.at[i]).wait()
    for d in range(NY):
        pltpu.make_async_copy(mine, mine, s_send.at[8 + d]).wait()
    for d in NEAR:
        pltpu.make_async_copy(mine, mine, s_send.at[d]).wait()
    for d in FAR:
        quarter = s_v.at[h, y, pl.ds(0, QUARTER)]
        pltpu.make_async_copy(quarter, quarter, s_send.at[d]).wait()
        three_quarters = s_v.at[h, y, pl.ds(0, BLOCK - QUARTER)]
        pltpu.make_async_copy(three_quarters, three_quarters, q_send.at[d]).wait()
    for p in range(2):
        for j in range(NY // 2):
            pair = c_send.at[p, pl.ds(0, 2)]
            pltpu.make_async_copy(pair, pair, c_sems.at[p, 0, j]).wait()
    for d in range(1, NY):
        pltpu.make_async_copy(f_y.at[h, y], f_y.at[h, y], f_sems.at[0, d]).wait()
        pltpu.make_async_copy(f_z.at[h, z], f_z.at[h, z], f_sems.at[0, 8 + d]).wait()
    for d in range(1, NX):
        pltpu.make_async_copy(f_x.at[h, x], f_x.at[h, x], f_sems.at[0, 16 + d]).wait()


def on_device(activations, sketch):
    rows_total = activations.shape[0] * lax.axis_size("row") * lax.axis_size("col")
    vmem = pltpu.VMEM
    shapes = [
        vmem((ROWS, K), f32), vmem((2, ROWS, NY * BLOCK), bf16), vmem((2, NY, BLOCK, K), bf16), vmem((ROWS, K), f32),
        vmem((2 * K, ROWS), bf16), vmem((K, 2 * K), f32), vmem((2, 2 * K, NY * BLOCK), bf16),
        vmem((2, 2 * NY, 8, K), f32), vmem((2, 2 * NY - 1, 8, K), f32),
        vmem((2, NZ, 8, K), f32), vmem((2, NX, 8, K), f32), vmem((2, 2 * NY, 8, K), f32),
        vmem((2, NY, K, BLOCK), bf16), vmem((2, NY, K, BLOCK), bf16),
        vmem((2, NY, 32, BLOCK), bf16), vmem((2, NZ, 64, K), bf16), vmem((2, NX, NY, 16, BLOCK), bf16),
        vmem((2, NY - 1, 32, BLOCK), bf16), vmem((2, NZ - 1, 64, K), bf16), vmem((2, NX - 1, NY, 16, BLOCK), bf16),
        vmem((NY, 8, 3 * K), f32), vmem((NZ, 8, 3 * K), f32), vmem((NY - 1, 8, 3 * K), f32), vmem((NZ - 1, 8, 3 * K), f32),
        vmem((NZ, 8, K), f32), vmem((NY, 8, K), f32), vmem((NY, 16, BLOCK), bf16),
        vmem((NZ - 1, 8, K), f32), vmem((NY - 1, 8, K), f32), vmem((NY - 1, 16, BLOCK), bf16),
        vmem((NX, 8, 2 * K), f32), vmem((NZ, 8, BLOCK), f32), vmem((NY, 8, BLOCK), f32),
        vmem((NY, 8, 3 * K), f32), vmem((NZ, 8, 3 * K), f32),
        vmem((NX, 8, K), f32), vmem((NX, 8, K), f32), vmem((NZ, 16, BLOCK), f32),
        vmem((2, NY, NZ, 8, K), f32), vmem((2, NZ, NY, 8, K), f32), vmem((2, NX, 2, NY, 8, BLOCK), f32),
        vmem((NZ, 8, K), f32), vmem((NZ, 8, K), f32), vmem((NX, 16, BLOCK), f32),
        pltpu.SemaphoreType.DMA((2,)), pltpu.SemaphoreType.DMA((16,)), pltpu.SemaphoreType.DMA((8,)),
        pltpu.SemaphoreType.DMA((8,)), pltpu.SemaphoreType.DMA((8,)), pltpu.SemaphoreType.DMA((8,)),
        pltpu.SemaphoreType.DMA((2, 2, NY // 2)), pltpu.SemaphoreType.DMA((2, 24)),
        pltpu.SemaphoreType.DMA((48,)), pltpu.SemaphoreType.DMA((48,)),
    ]
    here = pl.BlockSpec(memory_space=pltpu.VMEM)
    far = pl.BlockSpec(memory_space=pltpu.HBM)
    return pl.pallas_call(
        functools.partial(kernel, math.sqrt(rows_total)),
        out_shape=(jax.ShapeDtypeStruct((ROWS, K), f32), jax.ShapeDtypeStruct((BLOCK, K), f32)),
        in_specs=[far, far],
        out_specs=(here, here),
        scratch_shapes=shapes,
        compiler_params=pltpu.CompilerParams(
            collective_id=0, has_side_effects=True, vmem_limit_bytes=52 << 20
        ),
        name="subspace",
    )(activations, sketch)


def solution(mesh):
    placed = (P(("row", "col"), None), P("col", None))
    return jax.shard_map(
        on_device,
        mesh=mesh,
        in_specs=placed,
        out_specs=(P(("row", "col"), None), P("col", None)),
        check_vma=False,
    )
```

```python
import functools
import math

import jax
import jax.numpy as jnp
from jax import lax
from jax.experimental import pallas as pl
from jax.experimental.pallas import tpu as pltpu
from jax.sharding import PartitionSpec as P

f32, bf16 = jnp.float32, jnp.bfloat16
NX, NY, NZ = 4, 8, 8
K, BLOCK, ROWS = 128, 256, 512
PIVOTS = 16
QUARTER = BLOCK // NX
NT = (((1,), (1,)), ((), ()))
RING8 = (4, 3, 5, 2, 6, 1, 7)
RING4 = (2, 1, 3)
NEAR, FAR = (1, 7, 2, 6), (4, 3, 5)
COL16 = (8, 7, 9, 6, 10, 5, 11, 4, 12, 3, 13, 2, 14, 1, 15)


def split2(value):
    high = value.astype(bf16)
    return high, (value - high.astype(f32)).astype(bf16)


def split3(value):
    high = value.astype(bf16)
    rest = value - high.astype(f32)
    middle = rest.astype(bf16)
    return high, middle, (rest - middle.astype(f32)).astype(bf16)


def times_transposed(left, right):
    lh, ll = split2(left)
    rh, rl = split2(right)
    return lax.dot_general(
        jnp.concatenate([lh, ll, lh], axis=1),
        jnp.concatenate([rh, rh, rl], axis=1),
        NT,
        preferred_element_type=f32,
    )


def cholesky_stage(b, work):
    base = pl.multiple_of(b * PIVOTS, PIVOTS)
    panel = work[pl.ds(base, PIVOTS), :]
    g, w = panel[:, :K], panel[:, K:]
    shape = (PIVOTS, K)
    lane = lax.broadcasted_iota(jnp.int32, shape, 1)
    sub = lax.broadcasted_iota(jnp.int32, shape, 0)

    def column(k):
        return jnp.broadcast_to(jnp.sum(jnp.where(lane == base + k, g, 0.0), axis=1, keepdims=True), shape)

    def row(value, i):
        return jnp.broadcast_to(value[i : i + 1], shape)

    pivots = [column(k) for k in range(PIVOTS)]
    for i in range(PIVOTS):
        r = lax.rsqrt(row(pivots[i], i))
        low = jnp.where(sub > i, pivots[i] * r, 0.0)
        gi, wi = row(g, i) * r, row(w, i) * r
        g = jnp.where(sub == i, gi, g - low * gi)
        w = jnp.where(sub == i, wi, w - low * wi)
        for k in range(i + 1, PIVOTS):
            pivots[k] = pivots[k] - low * (row(pivots[k], i) * r)
    rows = jnp.concatenate([g, w], axis=1)
    work[pl.ds(base, PIVOTS), :] = rows
    left = split3(jnp.where(lane >= base + PIVOTS, g, 0.0))
    right = split3(rows)
    pairs = ((0, 0), (0, 1), (1, 0), (1, 1), (0, 2), (2, 0))
    work[...] -= lax.dot_general(
        jnp.concatenate([left[i] for i, _ in pairs], axis=0),
        jnp.concatenate([right[j] for _, j in pairs], axis=0),
        (((0,), (0,)), ((), ())),
        preferred_element_type=f32,
    )


def kernel(
    scale_root, a_hbm, s_hbm, basis, components,
    sec, a_v, s_v, f_acc, ft, work, coeffs,
    g_local, g_col, g_z, g_x, g_all,
    c_send, c_recv,
    y1s, z1s, x1s, y1r, z1r, x1r,
    over_y, over_z, over_y_in, over_z_in, y2s, z2s, x2s, y2r, z2r, x2r,
    yz3, v3, w3, y_full, z_full, y3, z3, x3, f_y, f_z, f_x, e_y, e_z, e_x,
    load_sem, s_send, s_recv, p_recv, q_send, q_recv, c_sems, f_sems, send_sems, recv_sems,
):
    row, col = lax.axis_index("row"), lax.axis_index("col")
    z, x, y, h = row // NX, lax.rem(row, NX), col // 2, lax.rem(col, 2)
    other = 1 - h

    def at(zz, xx, yy, hh):
        return (zz * NX + xx, yy * 2 + hh)

    def ring(axis):
        if axis == "y":
            return [(d, lax.rem(y + d, NY), at(z, x, lax.rem(y + d, NY), h)) for d in RING8]
        if axis == "col":
            spots = [lax.rem(col + d, 2 * NY) for d in COL16]
            return [(d, c, (row, c)) for d, c in zip(COL16, spots)]
        if axis == "z":
            return [(d, lax.rem(z + d, NZ), at(lax.rem(z + d, NZ), x, y, h)) for d in RING8]
        return [(d, lax.rem(x + d, NX), at(z, lax.rem(x + d, NX), y, h)) for d in RING4]

    partner = at(z, x, y, other)

    def columns(half, place):
        return a_v[half, :, pl.ds(pl.multiple_of(place * BLOCK, BLOCK), BLOCK)]

    pending = []
    slots = {}

    def slot(name):
        return slots.setdefault(name, len(slots))

    def copy_to(name, device, src, dst):
        i = slot(name)
        pltpu.make_async_remote_copy(
            src_ref=src, dst_ref=dst, send_sem=send_sems.at[i], recv_sem=recv_sems.at[i],
            device_id=device, device_id_type=pl.DeviceIdType.MESH,
        ).start()

    def arrived(name, ref):
        pltpu.make_async_copy(ref, ref, recv_sems.at[slot(name)]).wait()
        pending.append((slot(name), ref))

    def scatter(name, axis, src, dst):
        for d, place, device in ring(axis):
            copy_to(name, device, src.at[place], dst.at[d - 1])

    def spread(name, axis, ref):
        for _, _, device in ring(axis):
            copy_to(name, device, ref, ref)

    loads = [
        pltpu.make_async_copy(
            a_hbm.at[:, pl.ds((yy * 2 + hh) * BLOCK, BLOCK)], a_v.at[hh, :, pl.ds(yy * BLOCK, BLOCK)], load_sem.at[0]
        )
        for hh in range(2)
        for yy in range(NY)
    ]
    own_sketch = pltpu.make_async_copy(s_hbm, s_v.at[h, y], load_sem.at[1])
    own_sketch.start()
    for load in loads:
        load.start()
    barrier = pltpu.get_barrier_semaphore()
    peers = [device for axis in ("col", "z", "x") for _, _, device in ring(axis)]
    for device in peers:
        pl.semaphore_signal(barrier, inc=1, device_id=device, device_id_type=pl.DeviceIdType.MESH)
    own_sketch.wait()
    pl.semaphore_wait(barrier, len(peers))

    def sketch_copy(block, device, sends, recvs, d):
        return pltpu.make_async_remote_copy(
            src_ref=block, dst_ref=block, send_sem=sends, recv_sem=recvs.at[d],
            device_id=device, device_id_type=pl.DeviceIdType.MESH,
        )

    mine = s_v.at[h, y]
    span = pl.ds(pl.multiple_of(x * QUARTER, QUARTER), QUARTER)
    for d in FAR:
        sketch_copy(s_v.at[h, y, span], at(z, x, lax.rem(y + d, NY), h), s_send.at[d], q_recv, d).start()
    for d in NEAR:
        sketch_copy(mine, at(z, x, lax.rem(y + d, NY), h), s_send.at[d], s_recv, d).start()

    def hand_on(d, place):
        sketch_copy(s_v.at[h, place], partner, s_send.at[8 + d], p_recv, d).start()

    def origin(d):
        return lax.rem(y + NY - d, NY)

    def come(ds, size):
        for d in ds:
            part = s_v.at[h, origin(d), pl.ds(0, size)]
            pltpu.make_async_copy(part, part, s_recv.at[d]).wait()
            hand_on(d, origin(d))

    def add(half, ds):
        blocks = [(half, origin(d)) for d in ds]
        f_acc[...] += sum(jnp.dot(columns(*b), s_v[b], preferred_element_type=f32) for b in blocks)

    def add_other(ds):
        for d in ds:
            block = s_v.at[other, origin(d)]
            pltpu.make_async_copy(block, block, p_recv.at[d]).wait()
        add(other, ds)

    hand_on(0, y)
    pltpu.make_async_copy(a_v, a_v, load_sem.at[0]).wait()
    f_acc[...] = jnp.dot(columns(h, y), s_v[h, y], preferred_element_type=f32)
    come(NEAR[:2], BLOCK)
    for d in FAR:
        quarter = s_v.at[h, origin(d), span]
        pltpu.make_async_copy(quarter, quarter, q_recv.at[d]).wait()
        for _, _, device in ring("x"):
            sketch_copy(quarter, device, q_send.at[d], s_recv, d).start()
    come(NEAR[2:], BLOCK)
    add(h, NEAR)
    add_other((0,) + NEAR)
    come(FAR, BLOCK - QUARTER)
    add(h, FAR)
    add_other(FAR)

    def project(p, tall):
        high, low = split2(tall.T)
        ft[:K, :] = high
        ft[K:, :] = low

        def gram_first():
            both = ft[...]
            square = lax.dot_general(both, both, NT, preferred_element_type=f32)
            gram = (square[:K, :K] + square[K:, K:]) + (square[:K, K:] + square[K:, :K])
            g_local[p] = gram.reshape(2 * NY, 8, K)
            scatter(f"gc{p}", "col", g_local.at[p], g_col.at[p])

        if p == 1:
            gram_first()

        @pl.loop(0, NY // 2)
        def _(j):
            for i in (2 * j, 2 * j + 1):
                both = jnp.dot(ft[...], columns(other, i), preferred_element_type=f32)
                c_send[p, i] = (both[:K] + both[K:]).astype(bf16)
            pair = pl.ds(2 * j, 2)
            pltpu.make_async_remote_copy(
                src_ref=c_send.at[p, pair], dst_ref=c_recv.at[p, pair],
                send_sem=c_sems.at[p, 0, j], recv_sem=c_sems.at[p, 1, j],
                device_id=partner, device_id_type=pl.DeviceIdType.MESH,
            ).start()

        if p == 0:
            gram_first()

        @pl.loop(0, NY // 2)
        def _(j):
            values = []
            for i in (2 * j, 2 * j + 1):
                both = jnp.dot(ft[...], columns(h, i), preferred_element_type=f32)
                values.append(both[:K] + both[K:])
            pair = c_recv.at[p, pl.ds(2 * j, 2)]
            pltpu.make_async_copy(pair, pair, c_sems.at[p, 1, j]).wait()
            values = [value + pair[i].astype(f32) for i, value in enumerate(values)]
            for place, value in zip((2 * j, 2 * j + 1), values):
                y1s[p, place] = value[:32].astype(bf16)
                for q in range(NX):
                    both = [value[r + 8 * q : r + 8 * q + 8] for r in (64, 96)]
                    x1s[p, q, place] = jnp.concatenate(both, axis=0).astype(bf16)
            for q in range(NZ):
                r, c = 32 + 8 * (q // 2), K * (q % 2)
                both = jnp.concatenate([value[r : r + 8, c : c + K] for value in values], axis=0)
                z1s[p, q, pl.ds(pl.multiple_of(j * 16, 16), 16)] = both.astype(bf16)

        scatter(f"x1{p}", "x", x1s.at[p], x1r.at[p])
        scatter(f"y1{p}", "y", y1s.at[p], y1r.at[p])
        scatter(f"z1{p}", "z", z1s.at[p], z1r.at[p])

    def gram_z(p):
        arrived(f"gc{p}", g_col.at[p])
        g_z[p, z] = g_local[p, col] + jnp.sum(g_col[p], axis=0)
        spread(f"gz{p}", "z", g_z.at[p, z])

    def gram_x(p):
        arrived(f"gz{p}", g_z.at[p, pl.ds(0, NZ - 1)])
        g_x[p, x] = jnp.sum(g_z[p], axis=0)
        spread(f"gx{p}", "x", g_x.at[p, x])

    def gram_back(p):
        arrived(f"gx{p}", g_x.at[p, pl.ds(0, NX - 1)])
        g_all[p, col] = jnp.sum(g_x[p], axis=0)
        spread(f"ga{p}", "col", g_all.at[p, col])

    def gram_done(p):
        arrived(f"ga{p}", g_all.at[p, pl.ds(0, 2 * NY - 1)])
        ri = lax.broadcasted_iota(jnp.int32, (K, K), 0)
        ci = lax.broadcasted_iota(jnp.int32, (K, K), 1)
        work[:, :K] = g_all[p].reshape(K, K)
        work[:, K:] = jnp.where(ri == ci, 1.0, 0.0)

    def stages(lo, hi):
        @pl.loop(lo, hi)
        def _(b):
            cholesky_stage(b, work)

    def total(own, parts):
        return own.astype(f32) + jnp.sum(parts.astype(f32), axis=0)

    def y_tiles(p):
        arrived(f"y1{p}", y1r.at[p])
        value = total(y1s[p, y], y1r[p])
        return [value[8 * (q // 2) : 8 * (q // 2) + 8, K * (q % 2) : K * (q % 2) + K] for q in range(NZ)]

    def z_tiles(p):
        arrived(f"z1{p}", z1r.at[p])
        return total(z1s[p, z], z1r[p]).reshape(NY, 8, K)

    def two_first():
        arrived("x10", x1r.at[0])
        value = total(x1s[0, x], x1r[0])
        for q, tile in enumerate(y_tiles(0)):
            over_z[q, :, :K] = tile
            over_z[q, :, K:] = value[q, 8:]
        scatter("wz", "z", over_z, over_z_in)
        over_y[:, :, :K] = z_tiles(0)
        over_y[:, :, K:] = value[:, :8]
        scatter("wy", "y", over_y, over_y_in)

    def three_first():
        arrived("wz", over_z_in)
        value = total(over_z[z], over_z_in[...])
        yz3[x, :, :K] = value[:, :K]
        w3[y] = value[:, K:]
        spread("w3", "y", w3.at[y])
        arrived("wy", over_y_in)
        value = total(over_y[y], over_y_in[...])
        yz3[x, :, K:] = value[:, :K]
        v3[z] = value[:, K:]
        spread("v3", "z", v3.at[z])
        spread("yz3", "x", yz3.at[x])

    def four_first():
        arrived("yz3", yz3.at[pl.ds(0, NX - 1)])
        value = jnp.sum(yz3[...], axis=0)
        arrived("w3", w3.at[pl.ds(0, NY - 1)])
        z_full[z, :, :K] = value[:, :K]
        z_full[z, :, K:] = jnp.sum(w3[...], axis=0)
        spread("z4", "z", z_full.at[z])
        arrived("v3", v3.at[pl.ds(0, NZ - 1)])
        y_full[y, :, :K] = value[:, K:]
        y_full[y, :, K:] = jnp.sum(v3[...], axis=0)
        spread("y4", "y", y_full.at[y])

    def two():
        arrived("x11", x1r.at[1])
        x2s[...] = total(x1s[1, x], x1r[1]).astype(bf16)
        scatter("x2", "y", x2s, x2r)
        for q, tile in enumerate(y_tiles(1)):
            y2s[q] = tile
        scatter("y2", "z", y2s, y2r)
        z2s[...] = z_tiles(1)
        scatter("z2", "y", z2s, z2r)

    def three():
        arrived("y2", y2r)
        y3[x] = total(y2s[z], y2r[...])
        spread("y3", "x", y3.at[x])
        arrived("z2", z2r)
        z3[x] = total(z2s[y], z2r[...])
        spread("z3", "x", z3.at[x])
        arrived("x2", x2r)
        x3[z] = total(x2s[y], x2r[...])
        spread("x3", "z", x3.at[z])

    project(0, f_acc[...])
    gram_z(0)
    two_first()
    gram_x(0)
    three_first()
    gram_back(0)
    four_first()
    arrived("z4", z_full.at[pl.ds(0, NZ - 1)])
    f_y[h, y] = z_full[:, :, :K]
    f_x[h, x, 1] = z_full[:, :, K:]
    arrived("y4", y_full.at[pl.ds(0, NY - 1)])
    f_z[h, z] = y_full[:, :, :K]
    f_x[h, x, 0] = y_full[:, :, K:]

    def fanned(i, block, device):
        pltpu.make_async_remote_copy(
            src_ref=block, dst_ref=block, send_sem=f_sems.at[0, i], recv_sem=f_sems.at[1, i],
            device_id=device, device_id_type=pl.DeviceIdType.MESH,
        ).start()

    for k, (d, _, device) in enumerate(ring("y")):
        fanned(d, f_y.at[h, y], device)
        fanned(8 + d, f_z.at[h, z], ring("z")[k][2])
        if k < NX - 1:
            d, _, device = ring("x")[k]
            fanned(16 + d, f_x.at[h, x], device)
    copy_to("y6", partner, f_y.at[h, y], f_y.at[h, y])
    copy_to("z6", partner, f_z.at[h, z], f_z.at[h, z])
    copy_to("x6", partner, f_x.at[h, x], f_x.at[h, x])
    gram_done(0)
    stages(0, K // PIVOTS)

    def fan_in(name, i, block):
        pltpu.make_async_copy(block, block, f_sems.at[1, i]).wait()
        copy_to(name, partner, block, block)

    for d in (1, 7, 2, 6, 3, 5, 4):
        fan_in("y6", d, f_y.at[h, lax.rem(y + NY - d, NY)])
        fan_in("z6", 8 + d, f_z.at[h, lax.rem(z + NZ - d, NZ)])
        if d in (7, 2, 6):
            e = {7: 1, 2: 3, 6: 2}[d]
            fan_in("x6", 16 + e, f_x.at[h, lax.rem(x + NX - e, NX)])

    def tiles(ref):
        rows = [jnp.concatenate([ref[2 * k], ref[2 * k + 1]], axis=1) for k in range(4)]
        return jnp.concatenate(rows, axis=0)

    def second_part(half):
        @pl.loop(0, NY)
        def _(i):
            parts = [tiles(f_y.at[half, i]), tiles(f_z.at[half, :, i])]
            parts += [f_x[half, q, k, i] for k in range(2) for q in range(NX)]
            high, low = split2(jnp.concatenate(parts, axis=0))
            span = pl.ds(pl.multiple_of(i * BLOCK, BLOCK), BLOCK)
            coeffs[half, :, span] = jnp.concatenate([high, low], axis=0)

        both = lax.dot_general(a_v[half], coeffs[half], NT, preferred_element_type=f32)
        return both[:, :K] + both[:, K:]

    f_acc[...] = second_part(h)
    arrived("y6", f_y.at[other])
    arrived("z6", f_z.at[other])
    arrived("x6", f_x.at[other])
    sec[...] = times_transposed(f_acc[...] + second_part(other), work[:, K:])

    project(1, sec[...])
    gram_z(1)
    gram_x(1)
    two()
    gram_back(1)
    three()
    arrived("y3", y3.at[pl.ds(0, NX - 1)])
    e_y[z] = jnp.sum(y3[...], axis=0)
    spread("y7", "z", e_y.at[z])
    arrived("z3", z3.at[pl.ds(0, NX - 1)])
    e_z[z] = jnp.sum(z3[...], axis=0)
    spread("z7", "z", e_z.at[z])
    gram_done(1)
    stages(0, 3)
    arrived("x3", x3.at[pl.ds(0, NZ - 1)])
    e_x[x] = jnp.sum(x3[...], axis=0)
    spread("x7", "x", e_x.at[x])
    stages(3, K // PIVOTS)
    inverse = work[:, K:]
    basis[...] = times_transposed(sec[...], inverse) * scale_root
    arrived("y7", e_y.at[pl.ds(0, NZ - 1)])
    arrived("z7", e_z.at[pl.ds(0, NZ - 1)])
    arrived("x7", e_x.at[pl.ds(0, NX - 1)])
    summed = jnp.concatenate([tiles(e_y), tiles(e_z)] + [e_x[q, k : k + 8] for k in (0, 8) for q in range(NX)], axis=0)
    components[...] = times_transposed(summed.T, inverse) / scale_root

    for i, ref in pending:
        pltpu.make_async_copy(ref, ref, send_sems.at[i]).wait()
    for d in range(NY):
        pltpu.make_async_copy(mine, mine, s_send.at[8 + d]).wait()
    for d in NEAR:
        pltpu.make_async_copy(mine, mine, s_send.at[d]).wait()
    for d in FAR:
        quarter = s_v.at[h, y, pl.ds(0, QUARTER)]
        pltpu.make_async_copy(quarter, quarter, s_send.at[d]).wait()
        three_quarters = s_v.at[h, y, pl.ds(0, BLOCK - QUARTER)]
        pltpu.make_async_copy(three_quarters, three_quarters, q_send.at[d]).wait()
    for p in range(2):
        for j in range(NY // 2):
            pair = c_send.at[p, pl.ds(0, 2)]
            pltpu.make_async_copy(pair, pair, c_sems.at[p, 0, j]).wait()
    for d in range(1, NY):
        pltpu.make_async_copy(f_y.at[h, y], f_y.at[h, y], f_sems.at[0, d]).wait()
        pltpu.make_async_copy(f_z.at[h, z], f_z.at[h, z], f_sems.at[0, 8 + d]).wait()
    for d in range(1, NX):
        pltpu.make_async_copy(f_x.at[h, x], f_x.at[h, x], f_sems.at[0, 16 + d]).wait()


def on_device(activations, sketch):
    rows_total = activations.shape[0] * lax.axis_size("row") * lax.axis_size("col")
    vmem = pltpu.VMEM
    shapes = [
        vmem((ROWS, K), f32), vmem((2, ROWS, NY * BLOCK), bf16), vmem((2, NY, BLOCK, K), bf16), vmem((ROWS, K), f32),
        vmem((2 * K, ROWS), bf16), vmem((K, 2 * K), f32), vmem((2, 2 * K, NY * BLOCK), bf16),
        vmem((2, 2 * NY, 8, K), f32), vmem((2, 2 * NY - 1, 8, K), f32),
        vmem((2, NZ, 8, K), f32), vmem((2, NX, 8, K), f32), vmem((2, 2 * NY, 8, K), f32),
        vmem((2, NY, K, BLOCK), bf16), vmem((2, NY, K, BLOCK), bf16),
        vmem((2, NY, 32, BLOCK), bf16), vmem((2, NZ, 64, K), bf16), vmem((2, NX, NY, 16, BLOCK), bf16),
        vmem((2, NY - 1, 32, BLOCK), bf16), vmem((2, NZ - 1, 64, K), bf16), vmem((2, NX - 1, NY, 16, BLOCK), bf16),
        vmem((NY, 8, 3 * K), f32), vmem((NZ, 8, 3 * K), f32), vmem((NY - 1, 8, 3 * K), f32), vmem((NZ - 1, 8, 3 * K), f32),
        vmem((NZ, 8, K), f32), vmem((NY, 8, K), f32), vmem((NY, 16, BLOCK), bf16),
        vmem((NZ - 1, 8, K), f32), vmem((NY - 1, 8, K), f32), vmem((NY - 1, 16, BLOCK), bf16),
        vmem((NX, 8, 2 * K), f32), vmem((NZ, 8, BLOCK), f32), vmem((NY, 8, BLOCK), f32),
        vmem((NY, 8, 3 * K), f32), vmem((NZ, 8, 3 * K), f32),
        vmem((NX, 8, K), f32), vmem((NX, 8, K), f32), vmem((NZ, 16, BLOCK), f32),
        vmem((2, NY, NZ, 8, K), f32), vmem((2, NZ, NY, 8, K), f32), vmem((2, NX, 2, NY, 8, BLOCK), f32),
        vmem((NZ, 8, K), f32), vmem((NZ, 8, K), f32), vmem((NX, 16, BLOCK), f32),
        pltpu.SemaphoreType.DMA((2,)), pltpu.SemaphoreType.DMA((16,)), pltpu.SemaphoreType.DMA((8,)),
        pltpu.SemaphoreType.DMA((8,)), pltpu.SemaphoreType.DMA((8,)), pltpu.SemaphoreType.DMA((8,)),
        pltpu.SemaphoreType.DMA((2, 2, NY // 2)), pltpu.SemaphoreType.DMA((2, 24)),
        pltpu.SemaphoreType.DMA((48,)), pltpu.SemaphoreType.DMA((48,)),
    ]
    here = pl.BlockSpec(memory_space=pltpu.VMEM)
    far = pl.BlockSpec(memory_space=pltpu.HBM)
    return pl.pallas_call(
        functools.partial(kernel, math.sqrt(rows_total)),
        out_shape=(jax.ShapeDtypeStruct((ROWS, K), f32), jax.ShapeDtypeStruct((BLOCK, K), f32)),
        in_specs=[far, far],
        out_specs=(here, here),
        scratch_shapes=shapes,
        compiler_params=pltpu.CompilerParams(
            collective_id=0, has_side_effects=True, vmem_limit_bytes=52 << 20
        ),
        name="subspace",
    )(activations, sketch)


def solution(mesh):
    placed = (P(("row", "col"), None), P("col", None))
    return jax.shard_map(
        on_device,
        mesh=mesh,
        in_specs=placed,
        out_specs=(P(("row", "col"), None), P("col", None)),
        check_vma=False,
    )
```

```python
import functools
import math

import jax
import jax.numpy as jnp
from jax import lax
from jax.experimental import pallas as pl
from jax.experimental.pallas import tpu as pltpu
from jax.sharding import PartitionSpec as P

f32, bf16 = jnp.float32, jnp.bfloat16
NX, NY, NZ = 4, 8, 8
K, BLOCK, ROWS = 128, 256, 512
PIVOTS = 16
QUARTER = BLOCK // NX
NT = (((1,), (1,)), ((), ()))
RING8 = (4, 3, 5, 2, 6, 1, 7)
RING4 = (2, 1, 3)
NEAR, FAR = (1, 7, 2, 6), (4, 3, 5)
COL16 = (8, 7, 9, 6, 10, 5, 11, 4, 12, 3, 13, 2, 14, 1, 15)


def split2(value):
    high = value.astype(bf16)
    return high, (value - high.astype(f32)).astype(bf16)


def split3(value):
    high = value.astype(bf16)
    rest = value - high.astype(f32)
    middle = rest.astype(bf16)
    return high, middle, (rest - middle.astype(f32)).astype(bf16)


def times_transposed(left, right):
    lh, ll = split2(left)
    rh, rl = split2(right)
    return lax.dot_general(
        jnp.concatenate([lh, ll, lh], axis=1),
        jnp.concatenate([rh, rh, rl], axis=1),
        NT,
        preferred_element_type=f32,
    )


def cholesky_stage(b, work):
    base = pl.multiple_of(b * PIVOTS, PIVOTS)
    panel = work[pl.ds(base, PIVOTS), :]
    g, w = panel[:, :K], panel[:, K:]
    shape = (PIVOTS, K)
    lane = lax.broadcasted_iota(jnp.int32, shape, 1)
    sub = lax.broadcasted_iota(jnp.int32, shape, 0)

    def column(k):
        return jnp.broadcast_to(jnp.sum(jnp.where(lane == base + k, g, 0.0), axis=1, keepdims=True), shape)

    def row(value, i):
        return jnp.broadcast_to(value[i : i + 1], shape)

    pivots = [column(k) for k in range(PIVOTS)]
    for i in range(PIVOTS):
        r = lax.rsqrt(row(pivots[i], i))
        low = jnp.where(sub > i, pivots[i] * r, 0.0)
        gi, wi = row(g, i) * r, row(w, i) * r
        g = jnp.where(sub == i, gi, g - low * gi)
        w = jnp.where(sub == i, wi, w - low * wi)
        for k in range(i + 1, PIVOTS):
            pivots[k] = pivots[k] - low * (row(pivots[k], i) * r)
    rows = jnp.concatenate([g, w], axis=1)
    work[pl.ds(base, PIVOTS), :] = rows
    left = split3(jnp.where(lane >= base + PIVOTS, g, 0.0))
    right = split3(rows)
    pairs = ((0, 0), (0, 1), (1, 0), (1, 1), (0, 2), (2, 0))
    work[...] -= lax.dot_general(
        jnp.concatenate([left[i] for i, _ in pairs], axis=0),
        jnp.concatenate([right[j] for _, j in pairs], axis=0),
        (((0,), (0,)), ((), ())),
        preferred_element_type=f32,
    )


def kernel(
    scale_root, a_hbm, s_hbm, basis, components,
    sec, a_v, s_v, f_acc, ft, work, coeffs,
    g_local, g_col, g_z, g_x, g_all,
    c_send, c_recv,
    y1s, z1s, x1s, y1r, z1r, x1r,
    over_y, over_z, over_y_in, over_z_in, y2s, z2s, x2s, y2r, z2r, x2r,
    yz3, v3, w3, y_full, z_full, y3, z3, x3, f_y, f_z, f_x, e_y, e_z, e_x,
    load_sem, s_send, s_recv, p_recv, q_send, q_recv, c_sems, f_sems, send_sems, recv_sems,
):
    row, col = lax.axis_index("row"), lax.axis_index("col")
    z, x, y, h = row // NX, lax.rem(row, NX), col // 2, lax.rem(col, 2)
    other = 1 - h

    def at(zz, xx, yy, hh):
        return (zz * NX + xx, yy * 2 + hh)

    def ring(axis):
        if axis == "y":
            return [(d, lax.rem(y + d, NY), at(z, x, lax.rem(y + d, NY), h)) for d in RING8]
        if axis == "col":
            spots = [lax.rem(col + d, 2 * NY) for d in COL16]
            return [(d, c, (row, c)) for d, c in zip(COL16, spots)]
        if axis == "z":
            return [(d, lax.rem(z + d, NZ), at(lax.rem(z + d, NZ), x, y, h)) for d in RING8]
        return [(d, lax.rem(x + d, NX), at(z, lax.rem(x + d, NX), y, h)) for d in RING4]

    partner = at(z, x, y, other)

    def columns(half, place):
        return a_v[half, :, pl.ds(pl.multiple_of(place * BLOCK, BLOCK), BLOCK)]

    pending = []
    slots = {}

    def slot(name):
        return slots.setdefault(name, len(slots))

    def copy_to(name, device, src, dst):
        i = slot(name)
        pltpu.make_async_remote_copy(
            src_ref=src, dst_ref=dst, send_sem=send_sems.at[i], recv_sem=recv_sems.at[i],
            device_id=device, device_id_type=pl.DeviceIdType.MESH,
        ).start()

    def arrived(name, ref):
        pltpu.make_async_copy(ref, ref, recv_sems.at[slot(name)]).wait()
        pending.append((slot(name), ref))

    def scatter(name, axis, src, dst):
        for d, place, device in ring(axis):
            copy_to(name, device, src.at[place], dst.at[d - 1])

    def spread(name, axis, ref):
        for _, _, device in ring(axis):
            copy_to(name, device, ref, ref)

    loads = [
        pltpu.make_async_copy(
            a_hbm.at[:, pl.ds((yy * 2 + hh) * BLOCK, BLOCK)], a_v.at[hh, :, pl.ds(yy * BLOCK, BLOCK)], load_sem.at[0]
        )
        for hh in range(2)
        for yy in range(NY)
    ]
    own_sketch = pltpu.make_async_copy(s_hbm, s_v.at[h, y], load_sem.at[1])
    own_sketch.start()
    for load in loads:
        load.start()
    barrier = pltpu.get_barrier_semaphore()
    peers = [device for axis in ("col", "z", "x") for _, _, device in ring(axis)]
    for device in peers:
        pl.semaphore_signal(barrier, inc=1, device_id=device, device_id_type=pl.DeviceIdType.MESH)
    own_sketch.wait()
    pl.semaphore_wait(barrier, len(peers))

    def sketch_copy(block, device, sends, recvs, d):
        return pltpu.make_async_remote_copy(
            src_ref=block, dst_ref=block, send_sem=sends, recv_sem=recvs.at[d],
            device_id=device, device_id_type=pl.DeviceIdType.MESH,
        )

    mine = s_v.at[h, y]
    span = pl.ds(pl.multiple_of(x * QUARTER, QUARTER), QUARTER)
    for d in FAR:
        sketch_copy(s_v.at[h, y, span], at(z, x, lax.rem(y + d, NY), h), s_send.at[d], q_recv, d).start()
    for d in NEAR:
        sketch_copy(mine, at(z, x, lax.rem(y + d, NY), h), s_send.at[d], s_recv, d).start()

    def hand_on(d, place):
        sketch_copy(s_v.at[h, place], partner, s_send.at[8 + d], p_recv, d).start()

    def origin(d):
        return lax.rem(y + NY - d, NY)

    def come(ds, size):
        for d in ds:
            part = s_v.at[h, origin(d), pl.ds(0, size)]
            pltpu.make_async_copy(part, part, s_recv.at[d]).wait()
            hand_on(d, origin(d))

    def add(half, ds):
        blocks = [(half, origin(d)) for d in ds]
        f_acc[...] += sum(jnp.dot(columns(*b), s_v[b], preferred_element_type=f32) for b in blocks)

    def add_other(ds):
        for d in ds:
            block = s_v.at[other, origin(d)]
            pltpu.make_async_copy(block, block, p_recv.at[d]).wait()
        add(other, ds)

    hand_on(0, y)
    pltpu.make_async_copy(a_v, a_v, load_sem.at[0]).wait()
    f_acc[...] = jnp.dot(columns(h, y), s_v[h, y], preferred_element_type=f32)
    come(NEAR[:2], BLOCK)
    for d in FAR:
        quarter = s_v.at[h, origin(d), span]
        pltpu.make_async_copy(quarter, quarter, q_recv.at[d]).wait()
        for _, _, device in ring("x"):
            sketch_copy(quarter, device, q_send.at[d], s_recv, d).start()
    come(NEAR[2:], BLOCK)
    add(h, NEAR)
    add_other((0,) + NEAR)
    come(FAR, BLOCK - QUARTER)
    add(h, FAR)
    add_other(FAR)

    def project(p, tall):
        high, low = split2(tall.T)
        ft[:K, :] = high
        ft[K:, :] = low

        def gram_first():
            both = ft[...]
            square = lax.dot_general(both, both, NT, preferred_element_type=f32)
            gram = (square[:K, :K] + square[K:, K:]) + (square[:K, K:] + square[K:, :K])
            g_local[p] = gram.reshape(2 * NY, 8, K)
            scatter(f"gc{p}", "col", g_local.at[p], g_col.at[p])

        if p == 1:
            gram_first()

        @pl.loop(0, NY // 2)
        def _(j):
            for i in (2 * j, 2 * j + 1):
                both = jnp.dot(ft[...], columns(other, i), preferred_element_type=f32)
                c_send[p, i] = (both[:K] + both[K:]).astype(bf16)
            pair = pl.ds(2 * j, 2)
            pltpu.make_async_remote_copy(
                src_ref=c_send.at[p, pair], dst_ref=c_recv.at[p, pair],
                send_sem=c_sems.at[p, 0, j], recv_sem=c_sems.at[p, 1, j],
                device_id=partner, device_id_type=pl.DeviceIdType.MESH,
            ).start()

        if p == 0:
            gram_first()

        @pl.loop(0, NY // 2)
        def _(j):
            values = []
            for i in (2 * j, 2 * j + 1):
                both = jnp.dot(ft[...], columns(h, i), preferred_element_type=f32)
                values.append(both[:K] + both[K:])
            pair = c_recv.at[p, pl.ds(2 * j, 2)]
            pltpu.make_async_copy(pair, pair, c_sems.at[p, 1, j]).wait()
            values = [value + pair[i].astype(f32) for i, value in enumerate(values)]
            for place, value in zip((2 * j, 2 * j + 1), values):
                y1s[p, place] = value[:32].astype(bf16)
                for q in range(NX):
                    both = [value[r + 8 * q : r + 8 * q + 8] for r in (64, 96)]
                    x1s[p, q, place] = jnp.concatenate(both, axis=0).astype(bf16)
            for q in range(NZ):
                r, c = 32 + 8 * (q // 2), K * (q % 2)
                both = jnp.concatenate([value[r : r + 8, c : c + K] for value in values], axis=0)
                z1s[p, q, pl.ds(pl.multiple_of(j * 16, 16), 16)] = both.astype(bf16)

        scatter(f"x1{p}", "x", x1s.at[p], x1r.at[p])
        scatter(f"y1{p}", "y", y1s.at[p], y1r.at[p])
        scatter(f"z1{p}", "z", z1s.at[p], z1r.at[p])

    def gram_z(p):
        arrived(f"gc{p}", g_col.at[p])
        g_z[p, z] = g_local[p, col] + jnp.sum(g_col[p], axis=0)
        spread(f"gz{p}", "z", g_z.at[p, z])

    def gram_x(p):
        arrived(f"gz{p}", g_z.at[p, pl.ds(0, NZ - 1)])
        g_x[p, x] = jnp.sum(g_z[p], axis=0)
        spread(f"gx{p}", "x", g_x.at[p, x])

    def gram_back(p):
        arrived(f"gx{p}", g_x.at[p, pl.ds(0, NX - 1)])
        g_all[p, col] = jnp.sum(g_x[p], axis=0)
        spread(f"ga{p}", "col", g_all.at[p, col])

    def gram_done(p):
        arrived(f"ga{p}", g_all.at[p, pl.ds(0, 2 * NY - 1)])
        ri = lax.broadcasted_iota(jnp.int32, (K, K), 0)
        ci = lax.broadcasted_iota(jnp.int32, (K, K), 1)
        work[:, :K] = g_all[p].reshape(K, K)
        work[:, K:] = jnp.where(ri == ci, 1.0, 0.0)

    def stages(lo, hi):
        @pl.loop(lo, hi)
        def _(b):
            cholesky_stage(b, work)

    def total(own, parts):
        return own.astype(f32) + jnp.sum(parts.astype(f32), axis=0)

    def y_tiles(p):
        arrived(f"y1{p}", y1r.at[p])
        value = total(y1s[p, y], y1r[p])
        return [value[8 * (q // 2) : 8 * (q // 2) + 8, K * (q % 2) : K * (q % 2) + K] for q in range(NZ)]

    def z_tiles(p):
        arrived(f"z1{p}", z1r.at[p])
        return total(z1s[p, z], z1r[p]).reshape(NY, 8, K)

    def two_first():
        arrived("x10", x1r.at[0])
        value = total(x1s[0, x], x1r[0])
        for q, tile in enumerate(y_tiles(0)):
            over_z[q, :, :K] = tile
            over_z[q, :, K:] = value[q, 8:]
        scatter("wz", "z", over_z, over_z_in)
        over_y[:, :, :K] = z_tiles(0)
        over_y[:, :, K:] = value[:, :8]
        scatter("wy", "y", over_y, over_y_in)

    def three_first():
        arrived("wz", over_z_in)
        value = total(over_z[z], over_z_in[...])
        yz3[x, :, :K] = value[:, :K]
        w3[y] = value[:, K:]
        spread("w3", "y", w3.at[y])
        arrived("wy", over_y_in)
        value = total(over_y[y], over_y_in[...])
        yz3[x, :, K:] = value[:, :K]
        v3[z] = value[:, K:]
        spread("v3", "z", v3.at[z])
        spread("yz3", "x", yz3.at[x])

    def four_first():
        arrived("yz3", yz3.at[pl.ds(0, NX - 1)])
        value = jnp.sum(yz3[...], axis=0)
        arrived("w3", w3.at[pl.ds(0, NY - 1)])
        z_full[z, :, :K] = value[:, :K]
        z_full[z, :, K:] = jnp.sum(w3[...], axis=0)
        spread("z4", "z", z_full.at[z])
        arrived("v3", v3.at[pl.ds(0, NZ - 1)])
        y_full[y, :, :K] = value[:, K:]
        y_full[y, :, K:] = jnp.sum(v3[...], axis=0)
        spread("y4", "y", y_full.at[y])

    def two():
        arrived("x11", x1r.at[1])
        x2s[...] = total(x1s[1, x], x1r[1]).astype(bf16)
        scatter("x2", "y", x2s, x2r)
        for q, tile in enumerate(y_tiles(1)):
            y2s[q] = tile
        scatter("y2", "z", y2s, y2r)
        z2s[...] = z_tiles(1)
        scatter("z2", "y", z2s, z2r)

    def three():
        arrived("y2", y2r)
        y3[x] = total(y2s[z], y2r[...])
        spread("y3", "x", y3.at[x])
        arrived("z2", z2r)
        z3[x] = total(z2s[y], z2r[...])
        spread("z3", "x", z3.at[x])
        arrived("x2", x2r)
        x3[z] = total(x2s[y], x2r[...])
        spread("x3", "z", x3.at[z])

    project(0, f_acc[...])
    gram_z(0)
    two_first()
    gram_x(0)
    three_first()
    gram_back(0)
    four_first()
    arrived("z4", z_full.at[pl.ds(0, NZ - 1)])
    f_y[h, y] = z_full[:, :, :K]
    f_x[h, x, 1] = z_full[:, :, K:]
    arrived("y4", y_full.at[pl.ds(0, NY - 1)])
    f_z[h, z] = y_full[:, :, :K]
    f_x[h, x, 0] = y_full[:, :, K:]

    def fanned(i, block, device):
        pltpu.make_async_remote_copy(
            src_ref=block, dst_ref=block, send_sem=f_sems.at[0, i], recv_sem=f_sems.at[1, i],
            device_id=device, device_id_type=pl.DeviceIdType.MESH,
        ).start()

    for k, (d, _, device) in enumerate(ring("y")):
        fanned(d, f_y.at[h, y], device)
        fanned(8 + d, f_z.at[h, z], ring("z")[k][2])
        if k < NX - 1:
            d, _, device = ring("x")[k]
            fanned(16 + d, f_x.at[h, x], device)
    copy_to("y6", partner, f_y.at[h, y], f_y.at[h, y])
    copy_to("z6", partner, f_z.at[h, z], f_z.at[h, z])
    copy_to("x6", partner, f_x.at[h, x], f_x.at[h, x])
    gram_done(0)
    stages(0, K // PIVOTS)

    def fan_in(name, i, block):
        pltpu.make_async_copy(block, block, f_sems.at[1, i]).wait()
        copy_to(name, partner, block, block)

    for d in (1, 7, 2, 6, 3, 5, 4):
        fan_in("y6", d, f_y.at[h, lax.rem(y + NY - d, NY)])
        fan_in("z6", 8 + d, f_z.at[h, lax.rem(z + NZ - d, NZ)])
        if d in (7, 2, 6):
            e = {7: 1, 2: 3, 6: 2}[d]
            fan_in("x6", 16 + e, f_x.at[h, lax.rem(x + NX - e, NX)])

    def tiles(ref):
        rows = [jnp.concatenate([ref[2 * k], ref[2 * k + 1]], axis=1) for k in range(4)]
        return jnp.concatenate(rows, axis=0)

    def second_part(half):
        @pl.loop(0, NY)
        def _(i):
            parts = [tiles(f_y.at[half, i]), tiles(f_z.at[half, :, i])]
            parts += [f_x[half, q, k, i] for k in range(2) for q in range(NX)]
            high, low = split2(jnp.concatenate(parts, axis=0))
            span = pl.ds(pl.multiple_of(i * BLOCK, BLOCK), BLOCK)
            coeffs[half, :, span] = jnp.concatenate([high, low], axis=0)

        both = lax.dot_general(a_v[half], coeffs[half], NT, preferred_element_type=f32)
        return both[:, :K] + both[:, K:]

    f_acc[...] = second_part(h)
    arrived("y6", f_y.at[other])
    arrived("z6", f_z.at[other])
    arrived("x6", f_x.at[other])
    sec[...] = times_transposed(f_acc[...] + second_part(other), work[:, K:])

    def left():
        for i, ref in pending:
            pltpu.make_async_copy(ref, ref, send_sems.at[i]).wait()
        pending.clear()

    def first_left():
        left()
        for d in range(NY):
            pltpu.make_async_copy(mine, mine, s_send.at[8 + d]).wait()
        for d in NEAR:
            pltpu.make_async_copy(mine, mine, s_send.at[d]).wait()
        for d in FAR:
            quarter = s_v.at[h, y, pl.ds(0, QUARTER)]
            pltpu.make_async_copy(quarter, quarter, s_send.at[d]).wait()
            three_quarters = s_v.at[h, y, pl.ds(0, BLOCK - QUARTER)]
            pltpu.make_async_copy(three_quarters, three_quarters, q_send.at[d]).wait()
        for p in range(2):
            for j in range(NY // 2):
                pair = c_send.at[p, pl.ds(0, 2)]
                pltpu.make_async_copy(pair, pair, c_sems.at[p, 0, j]).wait()
        for d in range(1, NY):
            pltpu.make_async_copy(f_y.at[h, y], f_y.at[h, y], f_sems.at[0, d]).wait()
            pltpu.make_async_copy(f_z.at[h, z], f_z.at[h, z], f_sems.at[0, 8 + d]).wait()
        for d in range(1, NX):
            pltpu.make_async_copy(f_x.at[h, x], f_x.at[h, x], f_sems.at[0, 16 + d]).wait()

    project(1, sec[...])
    gram_z(1)
    first_left()
    gram_x(1)
    two()
    gram_back(1)
    three()
    arrived("y3", y3.at[pl.ds(0, NX - 1)])
    e_y[z] = jnp.sum(y3[...], axis=0)
    spread("y7", "z", e_y.at[z])
    arrived("z3", z3.at[pl.ds(0, NX - 1)])
    e_z[z] = jnp.sum(z3[...], axis=0)
    spread("z7", "z", e_z.at[z])
    left()
    gram_done(1)
    stages(0, 3)
    arrived("x3", x3.at[pl.ds(0, NZ - 1)])
    e_x[x] = jnp.sum(x3[...], axis=0)
    spread("x7", "x", e_x.at[x])
    stages(3, K // PIVOTS)
    inverse = work[:, K:]
    basis[...] = times_transposed(sec[...], inverse) * scale_root
    arrived("y7", e_y.at[pl.ds(0, NZ - 1)])
    arrived("z7", e_z.at[pl.ds(0, NZ - 1)])
    arrived("x7", e_x.at[pl.ds(0, NX - 1)])
    summed = jnp.concatenate([tiles(e_y), tiles(e_z)] + [e_x[q, k : k + 8] for k in (0, 8) for q in range(NX)], axis=0)
    components[...] = times_transposed(summed.T, inverse) / scale_root

    left()


def on_device(activations, sketch):
    rows_total = activations.shape[0] * lax.axis_size("row") * lax.axis_size("col")
    vmem = pltpu.VMEM
    shapes = [
        vmem((ROWS, K), f32), vmem((2, ROWS, NY * BLOCK), bf16), vmem((2, NY, BLOCK, K), bf16), vmem((ROWS, K), f32),
        vmem((2 * K, ROWS), bf16), vmem((K, 2 * K), f32), vmem((2, 2 * K, NY * BLOCK), bf16),
        vmem((2, 2 * NY, 8, K), f32), vmem((2, 2 * NY - 1, 8, K), f32),
        vmem((2, NZ, 8, K), f32), vmem((2, NX, 8, K), f32), vmem((2, 2 * NY, 8, K), f32),
        vmem((2, NY, K, BLOCK), bf16), vmem((2, NY, K, BLOCK), bf16),
        vmem((2, NY, 32, BLOCK), bf16), vmem((2, NZ, 64, K), bf16), vmem((2, NX, NY, 16, BLOCK), bf16),
        vmem((2, NY - 1, 32, BLOCK), bf16), vmem((2, NZ - 1, 64, K), bf16), vmem((2, NX - 1, NY, 16, BLOCK), bf16),
        vmem((NY, 8, 3 * K), f32), vmem((NZ, 8, 3 * K), f32), vmem((NY - 1, 8, 3 * K), f32), vmem((NZ - 1, 8, 3 * K), f32),
        vmem((NZ, 8, K), f32), vmem((NY, 8, K), f32), vmem((NY, 16, BLOCK), bf16),
        vmem((NZ - 1, 8, K), f32), vmem((NY - 1, 8, K), f32), vmem((NY - 1, 16, BLOCK), bf16),
        vmem((NX, 8, 2 * K), f32), vmem((NZ, 8, BLOCK), f32), vmem((NY, 8, BLOCK), f32),
        vmem((NY, 8, 3 * K), f32), vmem((NZ, 8, 3 * K), f32),
        vmem((NX, 8, K), f32), vmem((NX, 8, K), f32), vmem((NZ, 16, BLOCK), f32),
        vmem((2, NY, NZ, 8, K), f32), vmem((2, NZ, NY, 8, K), f32), vmem((2, NX, 2, NY, 8, BLOCK), f32),
        vmem((NZ, 8, K), f32), vmem((NZ, 8, K), f32), vmem((NX, 16, BLOCK), f32),
        pltpu.SemaphoreType.DMA((2,)), pltpu.SemaphoreType.DMA((16,)), pltpu.SemaphoreType.DMA((8,)),
        pltpu.SemaphoreType.DMA((8,)), pltpu.SemaphoreType.DMA((8,)), pltpu.SemaphoreType.DMA((8,)),
        pltpu.SemaphoreType.DMA((2, 2, NY // 2)), pltpu.SemaphoreType.DMA((2, 24)),
        pltpu.SemaphoreType.DMA((48,)), pltpu.SemaphoreType.DMA((48,)),
    ]
    here = pl.BlockSpec(memory_space=pltpu.VMEM)
    far = pl.BlockSpec(memory_space=pltpu.HBM)
    return pl.pallas_call(
        functools.partial(kernel, math.sqrt(rows_total)),
        out_shape=(jax.ShapeDtypeStruct((ROWS, K), f32), jax.ShapeDtypeStruct((BLOCK, K), f32)),
        in_specs=[far, far],
        out_specs=(here, here),
        scratch_shapes=shapes,
        compiler_params=pltpu.CompilerParams(
            collective_id=0, has_side_effects=True, vmem_limit_bytes=52 << 20
        ),
        name="subspace",
    )(activations, sketch)


def solution(mesh):
    placed = (P(("row", "col"), None), P("col", None))
    return jax.shard_map(
        on_device,
        mesh=mesh,
        in_specs=placed,
        out_specs=(P(("row", "col"), None), P("col", None)),
        check_vma=False,
    )
```
